512 devices in a mesh: ctx: 16 (over y, core), tp: 32 (over x, z).
Axes of the slice: x: 4, y: 8, z: 8, core: 2. Of those that a mesh axis runs over, the one named last changes fastest.
Arguments:
- queries: bfloat16 [16384, 8192], P('ctx', 'tp'), may hold values from -30 to 30
- keys: bfloat16 [16384, 1024], P('ctx', 'tp'), may hold values from -30 to 30
- values: bfloat16 [16384, 1024], P('ctx', 'tp'), may hold values from -6 to 6
- grad_out: bfloat16 [16384, 8192], P('ctx', 'tp'), may hold values from -24 to 24
- doc_lengths: int32 [32], replicated, may hold values from 1 to 1024, 16384 in all
Outputs:
- attention_out: bfloat16 [16384, 8192], P('ctx', 'tp')
- grad_queries: bfloat16 [16384, 8192], P('ctx', 'tp')
- grad_keys: bfloat16 [16384, 1024], P('ctx', 'tp')
- grad_values: bfloat16 [16384, 1024], P('ctx', 'tp')
The draws below stay inside these ranges and needn't reach their ends.
All inputs are finite; a program needn't handle non-finite values.
Results may differ from the reference program's by a relative error of at most 0.025.
Values may be sent and summed in bfloat16 or wider, within the bound.
A program may use at most 128 MiB of HBM per device.

```python
import math
import jax
import jax.numpy as jnp
import numpy as np
from jax import lax

HEADS = 64
KVH = 8
HD = 128
TOK_DEV = 1024
DOCMAX = 1024
LENGTH = 16384
NDOCS = 32


def shared_rows(key):
    base_rows = jnp.clip(jax.random.normal(jax.random.fold_in(key, 11), (LENGTH, KVH * HD), jnp.float32), -6.0, 6.0)
    return base_rows


def draw_keys(key, part):
    base_rows = shared_rows(key)
    key_rows = base_rows
    return key_rows.astype(jnp.bfloat16)


def draw_queries(key, part):
    key = jax.random.fold_in(key, 5)
    query_rows = jnp.clip(jax.random.normal(key, (LENGTH, HEADS * HD), jnp.float32), -6.0, 6.0)
    return query_rows.astype(jnp.bfloat16)


def levels(rng, shape, shards, low, top_value):
    factor_of = 1.0
    for position, blocks in shards:
        heights = jax.random.uniform(jax.random.fold_in(jax.random.fold_in(rng, 6), position), (blocks,), jnp.float32, low / len(shards), top_value / len(shards))
        factor_of = factor_of * jnp.repeat(jnp.exp(heights), shape[position] // blocks).reshape((-1,) + (1,) * (len(shape) - 1 - position))
    return factor_of


def split_up(number_of, total, bound, skew):
    weights = [(1 << 20) // math.isqrt(standing ** skew) + 1 for standing in range(2, number_of + 1)]
    spare, given = total - bound - (number_of - 1), [1] * (number_of - 1)
    while spare > 0:
        movable = [i for i in range(number_of - 1) if given[i] < bound]
        pool, remaining = sum([weights[i] for i in movable]), spare
        for i in movable:
            addition = min(bound - given[i], max(1, remaining * weights[i] // pool), spare)
            given[i] = given[i] + addition
            spare = spare - addition
    return np.array([bound] + given)


def ragged_sizes(rng, count, total, bound, slope):
    if count == 2:
        one = jax.random.randint(rng, (), max(1, total - bound), min(bound, total - 1) + 1)
        return jnp.stack([one, total - one])
    lengths = jnp.asarray(split_up(count, total, bound, slope), jnp.int32)
    pairs = (count - 1) // 2
    donor, receiver = lengths[1:1 + 2 * pairs:2], lengths[2:2 + 2 * pairs:2]
    room = jnp.minimum(donor - 1, bound - receiver)
    shifted = jax.random.randint(jax.random.fold_in(rng, 1), (pairs,), 0, 1 << 20) % (room + 1)
    lengths = lengths.at[1:1 + 2 * pairs:2].set(donor - shifted).at[2:2 + 2 * pairs:2].set(receiver + shifted)
    return lengths[jax.random.permutation(jax.random.fold_in(rng, 2), count)]


def centred(rng, shape, spread, limit, split=(), kind=jnp.bfloat16):
    drawn = spread * jax.random.normal(rng, shape, jnp.float32)
    if split:
        drawn = drawn * levels(rng, shape, split, -0.22, 0.18)
    return jnp.clip(drawn, -limit, limit).astype(kind)


def setup_inputs(seed: int = 0) -> dict:
    splits = jax.random.split(jax.random.key(seed), 6)
    queries = draw_queries(jax.random.fold_in(splits[5], 71), 0)
    keys = draw_keys(jax.random.fold_in(splits[5], 71), 0)
    values = centred(splits[2], (LENGTH, KVH * HD), 1.0, 6.0, ((0, 16), (1, 32)))
    grad_out = centred(splits[3], (LENGTH, HEADS * HD), 4.0, 24.0, ((0, 16), (1, 32)))
    doc_lengths = ragged_sizes(splits[4], NDOCS, LENGTH, DOCMAX, 2).astype(jnp.int32)
    return dict(queries=queries, keys=keys, values=values, grad_out=grad_out, doc_lengths=doc_lengths)


NEG_FILL = -1e+30

def reference(queries, keys, values, grad_out, doc_lengths):
    length = queries.shape[0]
    block_len = min(512, TOK_DEV)
    key_span = DOCMAX + block_len
    group_size = HEADS // KVH
    score_scale = 1.0 / math.sqrt(HD)
    highest_prec = lax.Precision.HIGHEST
    doc_ends = jnp.cumsum(doc_lengths).astype(jnp.int32)
    positions = jnp.arange(length, dtype=jnp.int32)
    segments = lax.optimization_barrier(jnp.sum((doc_ends[None, :] <= positions[:, None]).astype(jnp.int32), axis=1))
    pad_pos = jnp.concatenate([jnp.arange(DOCMAX, dtype=jnp.int32) - DOCMAX, positions])
    pad_seg = jnp.concatenate([jnp.full((DOCMAX,), -1, jnp.int32), segments])
    zero_rows = jnp.zeros((DOCMAX, KVH * HD), keys.dtype)
    key_pad = jnp.concatenate([zero_rows, keys], axis=0)
    value_pad = jnp.concatenate([zero_rows, values], axis=0)

    def one_block(index, state_tuple):
        attention_out, grad_queries, kv_grads = state_tuple
        row_start = (index * block_len).astype(jnp.int32)
        query_block = lax.dynamic_slice_in_dim(queries, row_start, block_len, 0).astype(jnp.float32).reshape(block_len, KVH, group_size, HD)
        grad_block = lax.dynamic_slice_in_dim(grad_out, row_start, block_len, 0).astype(jnp.float32).reshape(block_len, KVH, group_size, HD)
        key_window = lax.dynamic_slice_in_dim(key_pad, row_start, key_span, 0).astype(jnp.float32).reshape(key_span, KVH, HD)
        value_window = lax.dynamic_slice_in_dim(value_pad, row_start, key_span, 0).astype(jnp.float32).reshape(key_span, KVH, HD)
        query_pos = lax.dynamic_slice_in_dim(positions, row_start, block_len, 0)
        query_seg = lax.dynamic_slice_in_dim(segments, row_start, block_len, 0)
        key_pos = lax.dynamic_slice_in_dim(pad_pos, row_start, key_span, 0)
        key_seg = lax.dynamic_slice_in_dim(pad_seg, row_start, key_span, 0)
        allowed = (query_seg[:, None] == key_seg[None, :]) & (key_pos[None, :] <= query_pos[:, None]) & (key_pos[None, :] >= 0)
        allowed = allowed[None, None]
        scores = jnp.einsum('qgjd,kgd->gjqk', query_block, key_window, precision=highest_prec) * score_scale
        scores = jnp.where(allowed, scores, NEG_FILL)
        row_max = lax.optimization_barrier(jnp.max(scores, axis=3, keepdims=True))
        log_total = row_max + jnp.log(lax.optimization_barrier(jnp.sum(jnp.where(allowed, jnp.exp(scores - row_max), 0.0), axis=3, keepdims=True)))
        prob_high = jnp.where(allowed, jnp.exp(scores - log_total), 0.0)
        prob_low = lax.optimization_barrier(prob_high.astype(jnp.bfloat16)).astype(jnp.float32)
        out_block = jnp.einsum('gjqk,kgd->qgjd', prob_low, value_window, precision=highest_prec).astype(jnp.bfloat16)
        row_delta = lax.optimization_barrier(jnp.sum(grad_block * out_block.astype(jnp.float32), axis=3))
        row_delta = jnp.transpose(row_delta, (1, 2, 0))[..., None]
        grad_prob = jnp.einsum('qgjd,kgd->gjqk', grad_block, value_window, precision=highest_prec)
        dscore = lax.optimization_barrier((prob_high * (grad_prob - row_delta) * score_scale).astype(jnp.bfloat16)).astype(jnp.float32)
        query_grad = jnp.einsum('gjqk,kgd->qgjd', dscore, key_window, precision=highest_prec)
        key_term = jnp.einsum('gjqk,qgjd->kgd', dscore, query_block, precision=highest_prec)
        value_term = jnp.einsum('gjqk,qgjd->kgd', prob_low, grad_block, precision=highest_prec)
        attention_out = lax.dynamic_update_slice_in_dim(attention_out, out_block.reshape(block_len, HEADS * HD), row_start, 0)
        grad_queries = lax.dynamic_update_slice_in_dim(grad_queries, query_grad.astype(jnp.bfloat16).reshape(block_len, HEADS * HD), row_start, 0)
        current = lax.dynamic_slice_in_dim(kv_grads, row_start, key_span, 1)
        added = jnp.stack([key_term, value_term]).reshape(2, key_span, KVH * HD)
        kv_grads = lax.dynamic_update_slice_in_dim(kv_grads, current + added, row_start, 1)
        return (attention_out, grad_queries, kv_grads)
    start_state = (jnp.zeros((length, HEADS * HD), jnp.bfloat16), jnp.zeros((length, HEADS * HD), jnp.bfloat16), jnp.zeros((2, DOCMAX + length, KVH * HD), jnp.float32))
    attention_out, grad_queries, kv_grads = lax.fori_loop(0, length // block_len, one_block, start_state)
    final_grads = kv_grads[:, DOCMAX:].astype(jnp.bfloat16)
    return (attention_out, grad_queries, final_grads[0], final_grads[1])
```

```python
import functools
import math

import jax
import jax.numpy as jnp
from jax import lax
from jax.experimental import pallas as pl
from jax.experimental.pallas import tpu as pltpu
from jax.sharding import PartitionSpec as P

HD = 128
BLK = 256
NEG_FILL = -1e30
MESH = pl.DeviceIdType.MESH


def dot(a, b):
    return jnp.dot(a, b, preferred_element_type=jnp.float32)


def kernel(
    n_ctx,
    tokens,
    share,
    doc_ref,
    q_hbm,
    kt_hbm,
    vt_hbm,
    do_hbm,
    out_hbm,
    dq_hbm,
    dkt_hbm,
    dvt_hbm,
    q_ref,
    do_ref,
    qt_ref,
    dot_ref,
    kv_ref,
    k_ref,
    v_ref,
    start_ref,
    s_ref,
    p_ref,
    out_ref,
    dq_ref,
    ret_send,
    ret_recv,
    total_ref,
    rs_send,
    rs_recv,
    fin_ref,
    load_sem,
    store_sem,
    g_send,
    g_recv,
    f_send,
    f_recv,
    b_send,
    b_recv,
    r_send,
    r_recv,
):
    scale = 1.0 / math.sqrt(HD)
    factor = scale * math.log2(math.e)
    ctx = lax.axis_index("ctx")
    tp = lax.axis_index("tp")
    place = lax.rem(tp, share)
    base = tp - place
    band = HD // share
    nxt = lax.rem(ctx + 1, n_ctx)
    prv = lax.rem(ctx + n_ctx - 1, n_ctx)
    span = tokens + BLK
    blocks = tokens // BLK
    own = pl.ds(tokens, tokens)
    before = pl.ds(0, tokens)
    kv_hbm = (kt_hbm, vt_hbm)

    def other(d):
        return lax.rem(place + d, share)

    def band_of(index):
        return pl.ds(pl.multiple_of(index * band, band), band)

    load_q = pltpu.make_async_copy(q_hbm, q_ref, load_sem.at[0])
    load_do = pltpu.make_async_copy(do_hbm, do_ref, load_sem.at[1])
    load_kv = [
        pltpu.make_async_copy(
            kv_hbm[i], kv_ref.at[i, band_of(place), own], load_sem.at[2 + i]
        )
        for i in range(2)
    ]
    for c in [load_q, load_do] + load_kv:
        c.start()

    barrier = pltpu.get_barrier_semaphore()
    for d in range(1, share):
        pl.semaphore_signal(
            barrier, inc=1, device_id=(ctx, base + other(d)), device_id_type=MESH
        )
    for c in (nxt, prv):
        pl.semaphore_signal(barrier, inc=1, device_id=(c, tp), device_id_type=MESH)
    pl.semaphore_wait(barrier, share + 1)

    def gather(i):
        copies = [
            pltpu.make_async_remote_copy(
                src_ref=kv_hbm[i],
                dst_ref=kv_ref.at[i, band_of(place), own],
                send_sem=g_send.at[i, d - 1],
                recv_sem=g_recv.at[i, d - 1],
                device_id=(ctx, base + other(d)),
                device_id_type=MESH,
            )
            for d in range(1, share)
        ]
        return copies

    def forward(i, d):
        which = lax.rem(place - d + share, share)
        src = kv_hbm[i] if d == 0 else kv_ref.at[i, band_of(which), own]
        return pltpu.make_async_remote_copy(
            src_ref=src,
            dst_ref=kv_ref.at[i, band_of(which), before],
            send_sem=f_send.at[i, d],
            recv_sem=f_recv.at[i, d],
            device_id=(nxt, tp),
            device_id_type=MESH,
        )

    gathers = [gather(i) for i in range(2)]
    forwards = [[forward(i, d) for d in range(share)] for i in range(2)]

    for c in gathers[0]:
        c.start()
    forwards[0][0].start()

    row_base = ctx * tokens
    window_base = row_base - tokens

    ends = []
    running = doc_ref[0]
    for k in range(1, doc_ref.shape[0]):
        ends.append(running)
        running = running + doc_ref[k]
    lane = lax.broadcasted_iota(jnp.int32, (128, 128), 1)
    sub = lax.broadcasted_iota(jnp.int32, (128, 128), 0)

    def find_start(chunk, carry):
        pos = sub + (row_base + chunk * 128)
        first = jnp.zeros((128, 128), jnp.int32)
        for e in ends:
            first = jnp.where(pos >= e, e, first)
        rows = pl.ds(pl.multiple_of(chunk * 128, 128), 128)
        start_ref[rows, :] = first - window_base - lane
        return carry

    lax.fori_loop(0, tokens // 128, find_start, 0)
    load_q.wait()
    qt_ref[...] = q_ref[...].T
    load_do.wait()
    dot_ref[...] = do_ref[...].T

    for d in range(1, share):
        gathers[0][d - 1].wait_recv()
        forwards[0][d].start()
    for c in gathers[1]:
        c.start()
    forwards[1][0].start()
    load_kv[0].wait()
    for d in range(share):
        forwards[0][d].wait_recv()

    lane32 = lax.broadcasted_iota(jnp.int32, (32, 128), 1)
    sub32 = lax.broadcasted_iota(jnp.int32, (32, 128), 0)

    def heads_of(ref, rows):
        return jnp.concatenate([ref[rows, 0:HD], ref[rows, HD : 2 * HD]], axis=0)

    def probabilities(b, carry):
        off = pl.multiple_of(b * BLK, BLK)
        rows = pl.ds(off, BLK)
        window = pl.ds(off, span)
        s_ref[...] = dot(heads_of(q_ref, rows), kv_ref[0, :, window])
        for r in range(0, 2 * BLK, 32):
            head, low = r // BLK, r % BLK
            these = pl.ds(off + low, 32)
            begin = start_ref[these, :] - off
            parts = []
            for j in range(span // 128):
                part = s_ref[r : r + 32, j * 128 : j * 128 + 128]
                ok = begin <= j * 128
                first = j * 128 - tokens
                if first + 127 > low:
                    ok = ok & (lane32 + first <= sub32 + low)
                parts.append(jnp.where(ok, part, NEG_FILL))
            scores = jnp.concatenate(parts, axis=1)
            top = jnp.max(scores, axis=1, keepdims=True)
            prob = jnp.exp2((scores - top) * factor)
            total = jnp.sum(prob, axis=1, keepdims=True)
            p_ref[head, these, window] = (prob * (1.0 / total)).astype(jnp.bfloat16)
        return carry

    lax.fori_loop(0, 1, probabilities, 0)
    k_ref[...] = kv_ref[0].T
    for d in range(1, share):
        gathers[1][d - 1].wait_recv()
        forwards[1][d].start()
    load_kv[1].wait()
    lax.fori_loop(1, blocks, probabilities, 0)

    left = (qt_ref, dot_ref)

    def column_sum(i, kc):
        first = max(0, kc - blocks)
        last = min(blocks - 1, kc)
        rows = slice(first * BLK, (last + 1) * BLK)
        cols = slice(kc * BLK, (kc + 1) * BLK)
        return dot(left[i][0:HD, rows], p_ref[0, rows, cols]) + dot(
            left[i][HD : 2 * HD, rows], p_ref[1, rows, cols]
        )

    def back(i, kc):
        cols = pl.ds(kc * BLK, BLK)
        return pltpu.make_async_remote_copy(
            src_ref=ret_send.at[i, :, cols],
            dst_ref=ret_recv.at[i, :, cols],
            send_sem=b_send.at[i, kc],
            recv_sem=b_recv.at[i, kc],
            device_id=(prv, tp),
            device_id_type=MESH,
        )

    backs = [[back(i, kc) for kc in range(blocks)] for i in range(2)]
    weights = (scale, 1.0)

    def send_back(i):
        for kc in range(blocks):
            cols = slice(kc * BLK, (kc + 1) * BLK)
            ret_send[i, :, cols] = (column_sum(i, kc) * weights[i]).astype(jnp.bfloat16)
            backs[i][kc].start()
        for kc in range(blocks):
            cols = slice(kc * BLK, (kc + 1) * BLK)
            total_ref[i, :, cols] = column_sum(i, kc + blocks) * weights[i]

    def scatter(i, d):
        return pltpu.make_async_remote_copy(
            src_ref=rs_send.at[i, band_of(other(d)), :],
            dst_ref=rs_recv.at[i, d - 1],
            send_sem=r_send.at[i, d - 1],
            recv_sem=r_recv.at[i, d - 1],
            device_id=(ctx, base + other(d)),
            device_id_type=MESH,
        )

    scatters = [[scatter(i, d) for d in range(1, share)] for i in range(2)]

    def add_and_scatter(i):
        for kc in range(blocks):
            cols = slice(kc * BLK, (kc + 1) * BLK)
            backs[i][kc].wait_recv()
            total = total_ref[i, :, cols] + ret_recv[i, :, cols].astype(jnp.float32)
            total_ref[i, :, cols] = total
            rs_send[i, :, cols] = total.astype(jnp.bfloat16)
        for c in scatters[i]:
            c.start()

    def finish(i):
        result = total_ref[i, band_of(place), :]
        for d in range(1, share):
            scatters[i][d - 1].wait_recv()
            result = result + rs_recv[i, d - 1].astype(jnp.float32)
        fin_ref[i] = result.astype(jnp.bfloat16)

    send_back(1)

    for d in range(share):
        forwards[1][d].wait_recv()
    v_ref[...] = kv_ref[1].T

    def score_grads(b, carry):
        off = pl.multiple_of(b * BLK, BLK)
        rows = pl.ds(off, BLK)
        window = pl.ds(off, span)
        prob = jnp.concatenate([p_ref[0, rows, window], p_ref[1, rows, window]], axis=0)
        low_out = dot(prob, v_ref[window, :]).astype(jnp.bfloat16)
        out_ref[rows, 0:HD] = low_out[0:BLK]
        out_ref[rows, HD : 2 * HD] = low_out[BLK : 2 * BLK]
        grads = heads_of(do_ref, rows)
        delta = jnp.sum(
            grads.astype(jnp.float32) * low_out.astype(jnp.float32), axis=1, keepdims=True
        )
        s_ref[...] = dot(grads, kv_ref[1, :, window])
        for r in range(0, 2 * BLK, 32):
            head, low = r // BLK, r % BLK
            these = pl.ds(off + low, 32)
            change = s_ref[r : r + 32, :] - delta[r : r + 32]
            held = p_ref[head, these, window].astype(jnp.float32)
            p_ref[head, these, window] = (held * change).astype(jnp.bfloat16)
        return carry

    lax.fori_loop(0, blocks // 2, score_grads, 0)
    add_and_scatter(1)
    lax.fori_loop(blocks // 2, blocks, score_grads, 0)
    store_out = pltpu.make_async_copy(out_ref, out_hbm, store_sem.at[0])
    store_out.start()

    send_back(0)

    def query_grads(b, carry):
        off = pl.multiple_of(b * BLK, BLK)
        rows = pl.ds(off, BLK)
        window = pl.ds(off, span)
        dscore = jnp.concatenate([p_ref[0, rows, window], p_ref[1, rows, window]], axis=0)
        low = (dot(dscore, k_ref[window, :]) * scale).astype(jnp.bfloat16)
        dq_ref[rows, 0:HD] = low[0:BLK]
        dq_ref[rows, HD : 2 * HD] = low[BLK : 2 * BLK]
        return carry

    lax.fori_loop(0, blocks // 2, query_grads, 0)
    add_and_scatter(0)
    lax.fori_loop(blocks // 2, blocks, query_grads, 0)
    store_dq = pltpu.make_async_copy(dq_ref, dq_hbm, store_sem.at[1])
    store_dq.start()

    finish(1)
    store_dv = pltpu.make_async_copy(fin_ref.at[1], dvt_hbm, store_sem.at[3])
    store_dv.start()
    finish(0)
    store_dk = pltpu.make_async_copy(fin_ref.at[0], dkt_hbm, store_sem.at[2])
    store_dk.start()

    for i in range(2):
        for c in gathers[i] + forwards[i] + backs[i] + scatters[i]:
            c.wait_send()
    for c in (store_out, store_dq, store_dv, store_dk):
        c.wait()


def on_device(queries, keys, values, grad_out, doc_lengths, *, n_ctx):
    tokens, width = queries.shape
    columns = keys.shape[1]
    share = HD // columns
    blocks = tokens // BLK
    bf16, f32 = jnp.bfloat16, jnp.float32
    anywhere = pl.BlockSpec(memory_space=pl.ANY)
    dma = pltpu.SemaphoreType.DMA
    out, dq, dkt, dvt = pl.pallas_call(
        functools.partial(kernel, n_ctx, tokens, share),
        out_shape=[
            jax.ShapeDtypeStruct((tokens, width), bf16),
            jax.ShapeDtypeStruct((tokens, width), bf16),
            jax.ShapeDtypeStruct((columns, tokens), bf16),
            jax.ShapeDtypeStruct((columns, tokens), bf16),
        ],
        in_specs=[pl.BlockSpec(memory_space=pltpu.SMEM)] + [anywhere] * 4,
        out_specs=[anywhere] * 4,
        scratch_shapes=[
            pltpu.VMEM((tokens, width), bf16),
            pltpu.VMEM((tokens, width), bf16),
            pltpu.VMEM((width, tokens), bf16),
            pltpu.VMEM((width, tokens), bf16),
            pltpu.VMEM((2, HD, 2 * tokens), bf16),
            pltpu.VMEM((2 * tokens, HD), bf16),
            pltpu.VMEM((2 * tokens, HD), bf16),
            pltpu.VMEM((tokens, 128), jnp.int32),
            pltpu.VMEM((2 * BLK, tokens + BLK), f32),
            pltpu.VMEM((2, tokens, 2 * tokens), bf16),
            pltpu.VMEM((tokens, width), bf16),
            pltpu.VMEM((tokens, width), bf16),
            pltpu.VMEM((2, HD, tokens), bf16),
            pltpu.VMEM((2, HD, tokens), bf16),
            pltpu.VMEM((2, HD, tokens), f32),
            pltpu.VMEM((2, HD, tokens), bf16),
            pltpu.VMEM((2, share - 1, columns, tokens), bf16),
            pltpu.VMEM((2, columns, tokens), bf16),
            dma((4,)),
            dma((4,)),
            dma((2, share - 1)),
            dma((2, share - 1)),
            dma((2, share)),
            dma((2, share)),
            dma((2, blocks)),
            dma((2, blocks)),
            dma((2, share - 1)),
            dma((2, share - 1)),
        ],
        compiler_params=pltpu.CompilerParams(
            collective_id=0, has_side_effects=True, vmem_limit_bytes=56 * 1024 * 1024
        ),
        cost_estimate=pl.CostEstimate(
            flops=6 * 2 * 2 * tokens * (tokens + BLK) * HD,
            bytes_accessed=4 * tokens * width * 2,
            transcendentals=2 * tokens * (tokens + BLK),
        ),
    )(doc_lengths, queries, keys.T, values.T, grad_out)
    return out, dq, dkt.T, dvt.T


def solution(mesh):
    in_specs = (P("ctx", "tp"), P("ctx", "tp"), P("ctx", "tp"), P("ctx", "tp"), P())
    out_specs = (P("ctx", "tp"), P("ctx", "tp"), P("ctx", "tp"), P("ctx", "tp"))
    return jax.shard_map(
        functools.partial(on_device, n_ctx=mesh.shape["ctx"]),
        mesh=mesh,
        in_specs=in_specs,
        out_specs=out_specs,
        check_vma=False,
    )
```

```python
import functools
import math

import jax
import jax.numpy as jnp
from jax import lax
from jax.experimental import pallas as pl
from jax.experimental.pallas import tpu as pltpu
from jax.sharding import PartitionSpec as P

HD = 128
BLK = 256
NEG_FILL = -1e30
MESH = pl.DeviceIdType.MESH


def dot(a, b):
    return jnp.dot(a, b, preferred_element_type=jnp.float32)


def kernel(
    n_ctx,
    tokens,
    share,
    doc_ref,
    q_hbm,
    kt_hbm,
    vt_hbm,
    do_hbm,
    out_ref,
    dq_ref,
    dkt_ref,
    dvt_ref,
    q_ref,
    do_ref,
    qt_ref,
    dot_ref,
    kv_ref,
    k_ref,
    v_ref,
    start_ref,
    s_ref,
    p_ref,
    delta_ref,
    max_ref,
    inv_ref,
    ret_send,
    ret_recv,
    total_ref,
    rs_send,
    rs_recv,
    load_sem,
    g_send,
    g_recv,
    f_send,
    f_recv,
    b_send,
    b_recv,
    r_send,
    r_recv,
):
    scale = 1.0 / math.sqrt(HD)
    factor = scale * math.log2(math.e)
    ctx = lax.axis_index("ctx")
    tp = lax.axis_index("tp")
    place = lax.rem(tp, share)
    base = tp - place
    band = HD // share
    nxt = lax.rem(ctx + 1, n_ctx)
    prv = lax.rem(ctx + n_ctx - 1, n_ctx)
    span = tokens + BLK
    blocks = tokens // BLK
    own = pl.ds(tokens, tokens)
    before = pl.ds(0, tokens)
    kv_hbm = (kt_hbm, vt_hbm)

    def other(d):
        return lax.rem(place + d, share)

    def band_of(index):
        return pl.ds(pl.multiple_of(index * band, band), band)

    load_q = pltpu.make_async_copy(q_hbm, q_ref, load_sem.at[0])
    load_do = pltpu.make_async_copy(do_hbm, do_ref, load_sem.at[1])
    load_kv = [
        pltpu.make_async_copy(
            kv_hbm[i], kv_ref.at[i, band_of(place), own], load_sem.at[2 + i]
        )
        for i in range(2)
    ]
    for c in [load_q, load_do] + load_kv:
        c.start()

    barrier = pltpu.get_barrier_semaphore()
    for d in range(1, share):
        pl.semaphore_signal(
            barrier, inc=1, device_id=(ctx, base + other(d)), device_id_type=MESH
        )
    for c in (nxt, prv):
        pl.semaphore_signal(barrier, inc=1, device_id=(c, tp), device_id_type=MESH)
    pl.semaphore_wait(barrier, share + 1)

    def gather(i):
        copies = [
            pltpu.make_async_remote_copy(
                src_ref=kv_hbm[i],
                dst_ref=kv_ref.at[i, band_of(place), own],
                send_sem=g_send.at[i, d - 1],
                recv_sem=g_recv.at[i, d - 1],
                device_id=(ctx, base + other(d)),
                device_id_type=MESH,
            )
            for d in range(1, share)
        ]
        return copies

    def forward(i, d):
        which = lax.rem(place - d + share, share)
        src = kv_hbm[i] if d == 0 else kv_ref.at[i, band_of(which), own]
        return pltpu.make_async_remote_copy(
            src_ref=src,
            dst_ref=kv_ref.at[i, band_of(which), before],
            send_sem=f_send.at[i, d],
            recv_sem=f_recv.at[i, d],
            device_id=(nxt, tp),
            device_id_type=MESH,
        )

    gathers = [gather(i) for i in range(2)]
    forwards = [[forward(i, d) for d in range(share)] for i in range(2)]

    for c in gathers[0]:
        c.start()
    forwards[0][0].start()

    row_base = ctx * tokens
    window_base = row_base - tokens

    ends = []
    running = doc_ref[0]
    for k in range(1, doc_ref.shape[0]):
        ends.append(running)
        running = running + doc_ref[k]
    lane = lax.broadcasted_iota(jnp.int32, (128, 128), 1)
    sub = lax.broadcasted_iota(jnp.int32, (128, 128), 0)

    def find_start(chunk, carry):
        pos = sub + (row_base + chunk * 128)
        first = jnp.zeros((128, 128), jnp.int32)
        for e in ends:
            first = jnp.where(pos >= e, e, first)
        rows = pl.ds(pl.multiple_of(chunk * 128, 128), 128)
        start_ref[rows, :] = first - window_base - lane
        return carry

    lax.fori_loop(0, tokens // 128, find_start, 0)
    load_q.wait()
    load_do.wait()

    for d in range(1, share):
        gathers[0][d - 1].wait_recv()
        forwards[0][d].start()
    for c in gathers[1]:
        c.start()
    forwards[1][0].start()
    load_kv[0].wait()
    for d in range(share):
        forwards[0][d].wait_recv()

    lane32 = lax.broadcasted_iota(jnp.int32, (32, 128), 1)
    sub32 = lax.broadcasted_iota(jnp.int32, (32, 128), 0)

    def heads_of(ref, rows):
        return jnp.concatenate([ref[rows, 0:HD], ref[rows, HD : 2 * HD]], axis=0)

    def score(b):
        rows, window = slice(b * BLK, b * BLK + BLK), slice(b * BLK, b * BLK + span)
        s_ref[b] = dot(heads_of(q_ref, rows), kv_ref[0, :, window])

    def masked(b, r, j, begin):
        low, first = r % BLK, j * 128 - tokens
        part = s_ref[b, r : r + 32, j * 128 : j * 128 + 128]
        ok = begin <= b * BLK + j * 128
        if first + 127 > low:
            ok = ok & (lane32 + first <= sub32 + low)
        return jnp.where(ok, part, NEG_FILL)

    def row_max(b):
        for r in range(0, 2 * BLK, 32):
            head, low = r // BLK, b * BLK + r % BLK
            begin = start_ref[low : low + 32, :]
            top = masked(b, r, 0, begin)
            for j in range(1, span // 128):
                top = jnp.maximum(top, masked(b, r, j, begin))
            top = jnp.max(top, axis=1, keepdims=True)
            max_ref[head, low : low + 32, :] = jnp.broadcast_to(top, (32, 128))

    def probabilities(b):
        for r in range(0, 2 * BLK, 32):
            head, low = r // BLK, b * BLK + r % BLK
            begin = start_ref[low : low + 32, :]
            top = max_ref[head, low : low + 32, :]
            total = jnp.zeros((32, 128), jnp.float32)
            for j in range(span // 128):
                prob = jnp.exp2((masked(b, r, j, begin) - top) * factor)
                total = total + prob
                cols = slice(b * BLK + j * 128, b * BLK + j * 128 + 128)
                p_ref[head, low : low + 32, cols] = prob.astype(jnp.bfloat16)
            inverse = 1.0 / jnp.sum(total, axis=1, keepdims=True)
            inv_ref[head, low : low + 32, :] = jnp.broadcast_to(inverse, (32, 128))

    def scaled_turned(src_ref, dst_ref, b):
        rows = slice(b * BLK, b * BLK + BLK)
        for h in range(2):
            cols = slice(h * HD, h * HD + HD)
            part = src_ref[rows, cols].astype(jnp.float32) * inv_ref[h, rows, :]
            dst_ref[cols, rows] = part.astype(jnp.bfloat16).T

    score(0)
    row_max(0)
    score(1)
    for b in range(blocks):
        if b + 2 < blocks:
            score(b + 2)
        if b + 1 < blocks:
            row_max(b + 1)
        probabilities(b)
        scaled_turned(do_ref, dot_ref, b)
        if b == 2:
            for d in range(1, share):
                gathers[1][d - 1].wait_recv()
                forwards[1][d].start()
            load_kv[1].wait()

    left = (qt_ref, dot_ref)
    weights = (scale, 1.0)

    def rows_of(kc):
        return range(max(0, kc - blocks), min(blocks - 1, kc) + 1)

    def column_sum(i, kc):
        rows = slice(rows_of(kc)[0] * BLK, rows_of(kc)[-1] * BLK + BLK)
        cols = slice(kc * BLK, (kc + 1) * BLK)
        total = dot(left[i][0:HD, rows], p_ref[0, rows, cols]) + dot(
            left[i][HD : 2 * HD, rows], p_ref[1, rows, cols]
        )
        return total * weights[i] if weights[i] != 1.0 else total

    def back(i, kc):
        cols = pl.ds(kc * BLK, BLK)
        return pltpu.make_async_remote_copy(
            src_ref=ret_send.at[i, :, cols],
            dst_ref=ret_recv.at[i, :, cols],
            send_sem=b_send.at[i, kc],
            recv_sem=b_recv.at[i, kc],
            device_id=(prv, tp),
            device_id_type=MESH,
        )

    def scatter(i, kc, d):
        cols = pl.ds(kc * BLK, BLK)
        return pltpu.make_async_remote_copy(
            src_ref=rs_send.at[i, band_of(other(d)), cols],
            dst_ref=rs_recv.at[i, d - 1, :, cols],
            send_sem=r_send.at[i, kc, d - 1],
            recv_sem=r_recv.at[i, kc, d - 1],
            device_id=(ctx, base + other(d)),
            device_id_type=MESH,
        )

    backs = [[back(i, kc) for kc in range(blocks)] for i in range(2)]
    scatters = [
        [[scatter(i, kc, d) for d in range(1, share)] for kc in range(blocks)] for i in range(2)
    ]

    def send_back(i, kc):
        ret_send[i, :, kc * BLK : (kc + 1) * BLK] = column_sum(i, kc).astype(jnp.bfloat16)
        backs[i][kc].start()

    def add_and_scatter(i, kc, mine):
        cols = slice(kc * BLK, (kc + 1) * BLK)
        backs[i][kc].wait_recv()
        total = mine + ret_recv[i, :, cols].astype(jnp.float32)
        total_ref[i, :, cols] = total
        rs_send[i, :, cols] = total.astype(jnp.bfloat16)
        for c in scatters[i][kc]:
            c.start()

    def finish(i):
        for kc in range(blocks):
            for c in scatters[i][kc]:
                c.wait_recv()
        result = total_ref[i, band_of(place), :]
        for d in range(1, share):
            result = result + rs_recv[i, d - 1].astype(jnp.float32)
        (dkt_ref, dvt_ref)[i][...] = result.astype(jnp.bfloat16)

    for kc in range(blocks):
        send_back(1, kc)
    for kc in range(blocks):
        total_ref[1, :, kc * BLK : (kc + 1) * BLK] = column_sum(1, kc + blocks)

    for d in range(share):
        forwards[1][d].wait_recv()
    v_ref[...] = kv_ref[1].T

    def outputs(b):
        rows, window = slice(b * BLK, b * BLK + BLK), slice(b * BLK, b * BLK + span)
        prob = jnp.concatenate([p_ref[0, rows, window], p_ref[1, rows, window]], axis=0)
        sums = dot(prob, v_ref[window, :])
        for h in range(2):
            part = (sums[h * BLK : h * BLK + BLK] * inv_ref[h, rows, :]).astype(jnp.bfloat16)
            out_ref[rows, h * HD : h * HD + HD] = part
            grads = do_ref[rows, h * HD : h * HD + HD].astype(jnp.float32)
            delta = jnp.sum(grads * part.astype(jnp.float32), axis=1, keepdims=True)
            delta_ref[h, rows, :] = jnp.broadcast_to(delta, (BLK, 128))

    for b in range(blocks):
        outputs(b)
        if b == 1:
            for kc in range(blocks):
                add_and_scatter(1, kc, total_ref[1, :, kc * BLK : (kc + 1) * BLK])

    k_ref[...] = kv_ref[0].T
    for b in range(blocks):
        scaled_turned(q_ref, qt_ref, b)

    def score_grads(b, kc):
        rows, cols = slice(b * BLK, b * BLK + BLK), slice(kc * BLK, kc * BLK + BLK)
        change = dot(heads_of(do_ref, rows), kv_ref[1, :, cols])
        for r in range(0, 2 * BLK, 64):
            head, low = r // BLK, r % BLK
            these = slice(b * BLK + low, b * BLK + low + 64)
            delta = delta_ref[head, these, :]
            delta = jnp.concatenate([delta] * (BLK // 128), axis=1)
            held = p_ref[head, these, cols].astype(jnp.float32)
            p_ref[head, these, cols] = (held * (change[r : r + 64] - delta)).astype(jnp.bfloat16)

    for kc in range(2 * blocks):
        for b in rows_of(kc):
            score_grads(b, kc)
        if kc < blocks:
            send_back(0, kc)
        else:
            add_and_scatter(0, kc - blocks, column_sum(0, kc))

    finish(1)

    for b in range(blocks):
        rows, window = slice(b * BLK, b * BLK + BLK), slice(b * BLK, b * BLK + span)
        dscore = jnp.concatenate([p_ref[0, rows, window], p_ref[1, rows, window]], axis=0)
        sums = dot(dscore, k_ref[window, :])
        for h in range(2):
            part = sums[h * BLK : h * BLK + BLK] * (inv_ref[h, rows, :] * scale)
            dq_ref[rows, h * HD : h * HD + HD] = part.astype(jnp.bfloat16)

    finish(0)

    for i in range(2):
        for c in gathers[i] + forwards[i] + backs[i] + sum(scatters[i], []):
            c.wait_send()


def hand_over(*refs):
    count = len(refs) // 2
    sems = refs[-1]
    copies = [
        pltpu.make_async_copy(refs[i], refs[count + i], sems.at[i]) for i in range(count)
    ]
    for c in copies:
        c.start()
    for c in copies:
        c.wait()


def on_device(queries, keys, values, grad_out, doc_lengths, *, n_ctx):
    tokens, width = queries.shape
    columns = keys.shape[1]
    share = HD // columns
    blocks = tokens // BLK
    bf16, f32 = jnp.bfloat16, jnp.float32
    anywhere = pl.BlockSpec(memory_space=pltpu.HBM)
    dma = pltpu.SemaphoreType.DMA
    shapes = [(tokens, width), (tokens, width), (columns, tokens), (columns, tokens)]
    results = pl.pallas_call(
        functools.partial(kernel, n_ctx, tokens, share),
        out_shape=[pltpu.VMEM(shape, bf16) for shape in shapes],
        in_specs=[pl.BlockSpec(memory_space=pltpu.SMEM)] + [anywhere] * 4,
        out_specs=[pl.BlockSpec(memory_space=pltpu.VMEM)] * 4,
        scratch_shapes=[
            pltpu.VMEM((tokens, width), bf16),
            pltpu.VMEM((tokens, width), bf16),
            pltpu.VMEM((width, tokens), bf16),
            pltpu.VMEM((width, tokens), bf16),
            pltpu.VMEM((2, HD, 2 * tokens), bf16),
            pltpu.VMEM((2 * tokens, HD), bf16),
            pltpu.VMEM((2 * tokens, HD), bf16),
            pltpu.VMEM((tokens, 128), jnp.int32),
            pltpu.VMEM((blocks, 2 * BLK, tokens + BLK), f32),
            pltpu.VMEM((2, tokens, 2 * tokens), bf16),
            pltpu.VMEM((2, tokens, 128), f32),
            pltpu.VMEM((2, tokens, 128), f32),
            pltpu.VMEM((2, tokens, 128), f32),
            pltpu.VMEM((2, HD, tokens), bf16),
            pltpu.VMEM((2, HD, tokens), bf16),
            pltpu.VMEM((2, HD, tokens), f32),
            pltpu.VMEM((2, HD, tokens), bf16),
            pltpu.VMEM((2, share - 1, columns, tokens), bf16),
            dma((4,)),
            dma((2, share - 1)),
            dma((2, share - 1)),
            dma((2, share)),
            dma((2, share)),
            dma((2, blocks)),
            dma((2, blocks)),
            dma((2, blocks, share - 1)),
            dma((2, blocks, share - 1)),
        ],
        compiler_params=pltpu.CompilerParams(
            collective_id=0, has_side_effects=True, vmem_limit_bytes=60 * 1024 * 1024
        ),
        cost_estimate=pl.CostEstimate(
            flops=6 * 2 * 2 * tokens * (tokens + BLK) * HD,
            bytes_accessed=4 * tokens * width * 2,
            transcendentals=2 * tokens * (tokens + BLK),
        ),
    )(doc_lengths, queries, keys.T, values.T, grad_out)
    out, dq, dkt, dvt = pl.pallas_call(
        hand_over,
        out_shape=[jax.ShapeDtypeStruct(shape, bf16) for shape in shapes],
        in_specs=[pl.BlockSpec(memory_space=pltpu.VMEM)] * 4,
        out_specs=[anywhere] * 4,
        scratch_shapes=[dma((4,))],
        compiler_params=pltpu.CompilerParams(vmem_limit_bytes=4 * 1024 * 1024),
        cost_estimate=pl.CostEstimate(
            flops=0, bytes_accessed=2 * tokens * width * 2, transcendentals=0
        ),
    )(*results)
    return out, dq, dkt.T, dvt.T


def solution(mesh):
    in_specs = (P("ctx", "tp"), P("ctx", "tp"), P("ctx", "tp"), P("ctx", "tp"), P())
    out_specs = (P("ctx", "tp"), P("ctx", "tp"), P("ctx", "tp"), P("ctx", "tp"))
    return jax.shard_map(
        functools.partial(on_device, n_ctx=mesh.shape["ctx"]),
        mesh=mesh,
        in_specs=in_specs,
        out_specs=out_specs,
        check_vma=False,
    )
```

```python
import functools
import math

import jax
import jax.numpy as jnp
from jax import lax
from jax.experimental import pallas as pl
from jax.experimental.pallas import tpu as pltpu
from jax.sharding import PartitionSpec as P

HD = 128
BLK = 256
NEG_FILL = -1e30
MESH = pl.DeviceIdType.MESH


def dot(a, b):
    return jnp.dot(a, b, preferred_element_type=jnp.float32)


def kernel(
    n_ctx,
    tokens,
    share,
    doc_ref,
    q_hbm,
    kt_hbm,
    vt_hbm,
    do_hbm,
    out_ref,
    dq_ref,
    dkt_ref,
    dvt_ref,
    q_ref,
    do_ref,
    qt_ref,
    dot_ref,
    kv_ref,
    k_ref,
    v_ref,
    start_ref,
    s_ref,
    p_ref,
    delta_ref,
    max_ref,
    inv_ref,
    ret_send,
    ret_recv,
    total_ref,
    rs_send,
    rs_recv,
    load_sem,
    g_send,
    g_recv,
    f_send,
    f_recv,
    b_send,
    b_recv,
    r_send,
    r_recv,
):
    scale = 1.0 / math.sqrt(HD)
    factor = scale * math.log2(math.e)
    ctx = lax.axis_index("ctx")
    tp = lax.axis_index("tp")
    place = lax.rem(tp, share)
    base = tp - place
    band = HD // share
    nxt = lax.rem(ctx + 1, n_ctx)
    prv = lax.rem(ctx + n_ctx - 1, n_ctx)
    span = tokens + BLK
    blocks = tokens // BLK
    own = pl.ds(tokens, tokens)
    before = pl.ds(0, tokens)
    kv_hbm = (kt_hbm, vt_hbm)

    in_middle = lax.rem((place + 1) // 2, 2) == 1
    others = (
        place,
        place + 1 - 2 * lax.rem(place, 2),
        place + 2 - 4 * (place // 2),
        share - 1 - place,
    )

    def other(d):
        return others[d]

    def band_of(index):
        return pl.ds(pl.multiple_of(index * band, band), band)

    load_q = pltpu.make_async_copy(q_hbm, q_ref, load_sem.at[0])
    load_do = pltpu.make_async_copy(do_hbm, do_ref, load_sem.at[1])
    load_kv = [
        pltpu.make_async_copy(
            kv_hbm[i], kv_ref.at[i, band_of(place), own], load_sem.at[2 + i]
        )
        for i in range(2)
    ]
    for c in [load_q, load_do] + load_kv:
        c.start()

    barrier = pltpu.get_barrier_semaphore()
    for d in range(1, share):
        pl.semaphore_signal(
            barrier, inc=1, device_id=(ctx, base + other(d)), device_id_type=MESH
        )
    for c in (nxt, prv):
        pl.semaphore_signal(barrier, inc=1, device_id=(c, tp), device_id_type=MESH)
    pl.semaphore_wait(barrier, share + 1)

    def gather(i, d, source):
        return pltpu.make_async_remote_copy(
            src_ref=kv_hbm[i] if source == 0 else kv_ref.at[i, band_of(other(2)), own],
            dst_ref=kv_ref.at[i, band_of(other(source)), own],
            send_sem=g_send.at[i, 3 if source else d - 1],
            recv_sem=g_recv.at[i, 2 if source else d - 1],
            device_id=(ctx, base + other(d)),
            device_id_type=MESH,
        )

    def forward(i, d):
        src = kv_hbm[i] if d == 0 else kv_ref.at[i, band_of(other(d)), own]
        return pltpu.make_async_remote_copy(
            src_ref=src,
            dst_ref=kv_ref.at[i, band_of(other(d)), before],
            send_sem=f_send.at[i, d],
            recv_sem=f_recv.at[i, d],
            device_id=(nxt, tp),
            device_id_type=MESH,
        )

    gathers = [[gather(i, d, 0) for d in range(1, share)] for i in range(2)]
    relays = [gather(i, 1, 2) for i in range(2)]
    forwards = [[forward(i, d) for d in range(share)] for i in range(2)]

    def send_own(i):
        gathers[i][1].start()
        pl.when(in_middle)(gathers[i][2].start)
        gathers[i][0].start()
        forwards[i][0].start()

    def receive(i, d):
        gathers[i][d - 1].wait_recv()
        if d == 2:
            pl.when(in_middle)(relays[i].start)
        forwards[i][d].start()

    send_own(0)

    row_base = ctx * tokens
    window_base = row_base - tokens

    ends = []
    running = doc_ref[0]
    for k in range(1, doc_ref.shape[0]):
        ends.append(running)
        running = running + doc_ref[k]
    lane = lax.broadcasted_iota(jnp.int32, (128, 128), 1)
    sub = lax.broadcasted_iota(jnp.int32, (128, 128), 0)

    def find_start(chunk, carry):
        pos = sub + (row_base + chunk * 128)
        first = jnp.zeros((128, 128), jnp.int32)
        for e in ends:
            first = jnp.where(pos >= e, e, first)
        rows = pl.ds(pl.multiple_of(chunk * 128, 128), 128)
        start_ref[rows, :] = first - window_base - lane
        return carry

    lax.fori_loop(0, tokens // 128, find_start, 0)
    load_q.wait()
    load_do.wait()

    receive(0, 2)
    receive(0, 1)
    send_own(1)
    receive(0, 3)
    load_kv[0].wait()
    for d in range(share):
        forwards[0][d].wait_recv()
    receive(1, 2)

    lane32 = lax.broadcasted_iota(jnp.int32, (32, 128), 1)
    sub32 = lax.broadcasted_iota(jnp.int32, (32, 128), 0)

    def heads_of(ref, rows):
        return jnp.concatenate([ref[rows, 0:HD], ref[rows, HD : 2 * HD]], axis=0)

    def score(b):
        rows, window = slice(b * BLK, b * BLK + BLK), slice(b * BLK, b * BLK + span)
        s_ref[b] = dot(heads_of(q_ref, rows), kv_ref[0, :, window])

    def masked(b, r, j, begin):
        low, first = r % BLK, j * 128 - tokens
        part = s_ref[b, r : r + 32, j * 128 : j * 128 + 128]
        ok = begin <= b * BLK + j * 128
        if first + 127 > low:
            ok = ok & (lane32 + first <= sub32 + low)
        return jnp.where(ok, part, NEG_FILL)

    def row_max(b):
        for r in range(0, 2 * BLK, 32):
            head, low = r // BLK, b * BLK + r % BLK
            begin = start_ref[low : low + 32, :]
            top = masked(b, r, 0, begin)
            for j in range(1, span // 128):
                top = jnp.maximum(top, masked(b, r, j, begin))
            top = jnp.max(top, axis=1, keepdims=True)
            max_ref[head, low : low + 32, :] = jnp.broadcast_to(top, (32, 128))

    def probabilities(b):
        for r in range(0, 2 * BLK, 32):
            head, low = r // BLK, b * BLK + r % BLK
            begin = start_ref[low : low + 32, :]
            top = max_ref[head, low : low + 32, :]
            total = jnp.zeros((32, 128), jnp.float32)
            for j in range(span // 128):
                prob = jnp.exp2((masked(b, r, j, begin) - top) * factor)
                total = total + prob
                cols = slice(b * BLK + j * 128, b * BLK + j * 128 + 128)
                p_ref[head, low : low + 32, cols] = prob.astype(jnp.bfloat16)
            inverse = 1.0 / jnp.sum(total, axis=1, keepdims=True)
            inv_ref[head, low : low + 32, :] = jnp.broadcast_to(inverse, (32, 128))

    def scaled_turned(src_ref, dst_ref, b):
        rows = slice(b * BLK, b * BLK + BLK)
        for h in range(2):
            cols = slice(h * HD, h * HD + HD)
            part = src_ref[rows, cols].astype(jnp.float32) * inv_ref[h, rows, :]
            dst_ref[cols, rows] = part.astype(jnp.bfloat16).T

    score(0)
    row_max(0)
    score(1)
    for b in range(blocks):
        if b + 2 < blocks:
            score(b + 2)
        if b + 1 < blocks:
            row_max(b + 1)
        probabilities(b)
        scaled_turned(do_ref, dot_ref, b)
        if b == 2:
            receive(1, 1)
            receive(1, 3)
            load_kv[1].wait()

    left = (qt_ref, dot_ref)
    weights = (scale, 1.0)

    def rows_of(kc):
        return range(max(0, kc - blocks), min(blocks - 1, kc) + 1)

    def column_sum(i, kc):
        rows = slice(rows_of(kc)[0] * BLK, rows_of(kc)[-1] * BLK + BLK)
        cols = slice(kc * BLK, (kc + 1) * BLK)
        total = dot(left[i][0:HD, rows], p_ref[0, rows, cols]) + dot(
            left[i][HD : 2 * HD, rows], p_ref[1, rows, cols]
        )
        return total * weights[i] if weights[i] != 1.0 else total

    def back(i, kc):
        cols = pl.ds(kc * BLK, BLK)
        return pltpu.make_async_remote_copy(
            src_ref=ret_send.at[i, :, cols],
            dst_ref=ret_recv.at[i, :, cols],
            send_sem=b_send.at[i, kc],
            recv_sem=b_recv.at[i, kc],
            device_id=(prv, tp),
            device_id_type=MESH,
        )

    def straight(i, kc):
        return i == 0 and kc == blocks - 1

    def scatter(i, kc, d):
        cols = pl.ds(kc * BLK, BLK)
        target, slot = (1, 3) if d == share else (d, d - 1)
        return pltpu.make_async_remote_copy(
            src_ref=rs_send.at[i, band_of(other(min(d, share - 1))), cols],
            dst_ref=rs_recv.at[i, slot, :, cols],
            send_sem=r_send.at[i, kc, slot],
            recv_sem=r_recv.at[i, kc, slot],
            device_id=(ctx, base + other(target)),
            device_id_type=MESH,
        )

    backs = [[back(i, kc) for kc in range(blocks)] for i in range(2)]
    scatters = [
        [[scatter(i, kc, d) for d in range(1, share + 1)] for kc in range(blocks)]
        for i in range(2)
    ]

    def send_back(i, kc):
        ret_send[i, :, kc * BLK : (kc + 1) * BLK] = column_sum(i, kc).astype(jnp.bfloat16)
        backs[i][kc].start()

    def add_and_scatter(i, kc, mine):
        cols = slice(kc * BLK, (kc + 1) * BLK)
        backs[i][kc].wait_recv()
        total = mine + ret_recv[i, :, cols].astype(jnp.float32)
        total_ref[i, :, cols] = total
        rs_send[i, :, cols] = total.astype(jnp.bfloat16)
        first, second, third, relay = scatters[i][kc]
        if straight(i, kc):
            second.start()
            third.start()
            first.start()
        else:

            @pl.when(in_middle)
            def _():
                third.start()

            @pl.when(jnp.logical_not(in_middle))
            def _():
                relay.start()
                second.start()

            first.start()

    def add_on_the_way(i, kc):
        if straight(i, kc):
            return
        cols = slice(kc * BLK, (kc + 1) * BLK)

        @pl.when(in_middle)
        def _():
            scatters[i][kc][3].wait_recv()
            total = total_ref[i, band_of(other(2)), cols]
            total = total + rs_recv[i, 3, :, cols].astype(jnp.float32)
            rs_send[i, band_of(other(2)), cols] = total.astype(jnp.bfloat16)
            scatters[i][kc][1].start()

    def finish(i):
        for kc in range(blocks):
            cols = slice(kc * BLK, (kc + 1) * BLK)

            def add_third(kc=kc, cols=cols):
                scatters[i][kc][2].wait_recv()
                total_ref[i, band_of(place), cols] += rs_recv[i, 2, :, cols].astype(jnp.float32)

            scatters[i][kc][0].wait_recv()
            scatters[i][kc][1].wait_recv()
            if straight(i, kc):
                add_third()
            else:
                pl.when(in_middle)(add_third)
        result = total_ref[i, band_of(place), :]
        for d in range(1, share - 1):
            result = result + rs_recv[i, d - 1].astype(jnp.float32)
        (dkt_ref, dvt_ref)[i][...] = result.astype(jnp.bfloat16)

    def all_sent(i):
        first = gathers[i][:2] + forwards[i] + backs[i]
        in_the_middle = [gathers[i][2], relays[i]]
        at_the_ends = []
        for kc in range(blocks):
            first += scatters[i][kc][:2]
            if straight(i, kc):
                first.append(scatters[i][kc][2])
            else:
                in_the_middle.append(scatters[i][kc][2])
                at_the_ends.append(scatters[i][kc][3])
        for c in first:
            c.wait_send()

        @pl.when(in_middle)
        def _():
            for c in in_the_middle:
                c.wait_send()

        @pl.when(jnp.logical_not(in_middle))
        def _():
            for c in at_the_ends:
                c.wait_send()

    for kc in range(blocks):
        send_back(1, kc)
    for kc in range(blocks):
        total_ref[1, :, kc * BLK : (kc + 1) * BLK] = column_sum(1, kc + blocks)

    for d in range(share):
        forwards[1][d].wait_recv()
    v_ref[...] = kv_ref[1].T

    def outputs(b):
        rows, window = slice(b * BLK, b * BLK + BLK), slice(b * BLK, b * BLK + span)
        prob = jnp.concatenate([p_ref[0, rows, window], p_ref[1, rows, window]], axis=0)
        sums = dot(prob, v_ref[window, :])
        for h in range(2):
            part = (sums[h * BLK : h * BLK + BLK] * inv_ref[h, rows, :]).astype(jnp.bfloat16)
            out_ref[rows, h * HD : h * HD + HD] = part
            grads = do_ref[rows, h * HD : h * HD + HD].astype(jnp.float32)
            delta = jnp.sum(grads * part.astype(jnp.float32), axis=1, keepdims=True)
            delta_ref[h, rows, :] = jnp.broadcast_to(delta, (BLK, 128))

    for b in range(blocks):
        outputs(b)
        if b == 1:
            for kc in range(blocks):
                add_and_scatter(1, kc, total_ref[1, :, kc * BLK : (kc + 1) * BLK])
    for kc in range(blocks):
        add_on_the_way(1, kc)

    k_ref[...] = kv_ref[0].T
    for b in range(blocks):
        scaled_turned(q_ref, qt_ref, b)

    def score_grads(b, kc):
        rows, cols = slice(b * BLK, b * BLK + BLK), slice(kc * BLK, kc * BLK + BLK)
        change = dot(heads_of(do_ref, rows), kv_ref[1, :, cols])
        for r in range(0, 2 * BLK, 64):
            head, low = r // BLK, r % BLK
            these = slice(b * BLK + low, b * BLK + low + 64)
            delta = delta_ref[head, these, :]
            delta = jnp.concatenate([delta] * (BLK // 128), axis=1)
            held = p_ref[head, these, cols].astype(jnp.float32)
            p_ref[head, these, cols] = (held * (change[r : r + 64] - delta)).astype(jnp.bfloat16)

    for kc in range(2 * blocks):
        for b in rows_of(kc):
            score_grads(b, kc)
        if kc < blocks:
            send_back(0, kc)
        else:
            add_and_scatter(0, kc - blocks, column_sum(0, kc))
            if kc > blocks:
                add_on_the_way(0, kc - blocks - 1)

    finish(1)

    for b in range(blocks):
        rows, window = slice(b * BLK, b * BLK + BLK), slice(b * BLK, b * BLK + span)
        dscore = jnp.concatenate([p_ref[0, rows, window], p_ref[1, rows, window]], axis=0)
        sums = dot(dscore, k_ref[window, :])
        for h in range(2):
            part = sums[h * BLK : h * BLK + BLK] * (inv_ref[h, rows, :] * scale)
            dq_ref[rows, h * HD : h * HD + HD] = part.astype(jnp.bfloat16)

    finish(0)

    for i in range(2):
        all_sent(i)


def hand_over(*refs):
    count = len(refs) // 2
    sems = refs[-1]
    copies = [
        pltpu.make_async_copy(refs[i], refs[count + i], sems.at[i]) for i in range(count)
    ]
    for c in copies:
        c.start()
    for c in copies:
        c.wait()


def on_device(queries, keys, values, grad_out, doc_lengths, *, n_ctx):
    tokens, width = queries.shape
    columns = keys.shape[1]
    share = HD // columns
    blocks = tokens // BLK
    bf16, f32 = jnp.bfloat16, jnp.float32
    anywhere = pl.BlockSpec(memory_space=pltpu.HBM)
    dma = pltpu.SemaphoreType.DMA
    shapes = [(tokens, width), (tokens, width), (columns, tokens), (columns, tokens)]
    results = pl.pallas_call(
        functools.partial(kernel, n_ctx, tokens, share),
        out_shape=[pltpu.VMEM(shape, bf16) for shape in shapes],
        in_specs=[pl.BlockSpec(memory_space=pltpu.SMEM)] + [anywhere] * 4,
        out_specs=[pl.BlockSpec(memory_space=pltpu.VMEM)] * 4,
        scratch_shapes=[
            pltpu.VMEM((tokens, width), bf16),
            pltpu.VMEM((tokens, width), bf16),
            pltpu.VMEM((width, tokens), bf16),
            pltpu.VMEM((width, tokens), bf16),
            pltpu.VMEM((2, HD, 2 * tokens), bf16),
            pltpu.VMEM((2 * tokens, HD), bf16),
            pltpu.VMEM((2 * tokens, HD), bf16),
            pltpu.VMEM((tokens, 128), jnp.int32),
            pltpu.VMEM((blocks, 2 * BLK, tokens + BLK), f32),
            pltpu.VMEM((2, tokens, 2 * tokens), bf16),
            pltpu.VMEM((2, tokens, 128), f32),
            pltpu.VMEM((2, tokens, 128), f32),
            pltpu.VMEM((2, tokens, 128), f32),
            pltpu.VMEM((2, HD, tokens), bf16),
            pltpu.VMEM((2, HD, tokens), bf16),
            pltpu.VMEM((2, HD, tokens), f32),
            pltpu.VMEM((2, HD, tokens), bf16),
            pltpu.VMEM((2, share, columns, tokens), bf16),
            dma((4,)),
            dma((2, share)),
            dma((2, share - 1)),
            dma((2, share)),
            dma((2, share)),
            dma((2, blocks)),
            dma((2, blocks)),
            dma((2, blocks, share)),
            dma((2, blocks, share)),
        ],
        compiler_params=pltpu.CompilerParams(
            collective_id=0, has_side_effects=True, vmem_limit_bytes=60 * 1024 * 1024
        ),
        cost_estimate=pl.CostEstimate(
            flops=6 * 2 * 2 * tokens * (tokens + BLK) * HD,
            bytes_accessed=4 * tokens * width * 2,
            transcendentals=2 * tokens * (tokens + BLK),
        ),
    )(doc_lengths, queries, keys.T, values.T, grad_out)
    out, dq, dkt, dvt = pl.pallas_call(
        hand_over,
        out_shape=[jax.ShapeDtypeStruct(shape, bf16) for shape in shapes],
        in_specs=[pl.BlockSpec(memory_space=pltpu.VMEM)] * 4,
        out_specs=[anywhere] * 4,
        scratch_shapes=[dma((4,))],
        compiler_params=pltpu.CompilerParams(vmem_limit_bytes=4 * 1024 * 1024),
        cost_estimate=pl.CostEstimate(
            flops=0, bytes_accessed=2 * tokens * width * 2, transcendentals=0
        ),
    )(*results)
    return out, dq, dkt.T, dvt.T


def solution(mesh):
    in_specs = (P("ctx", "tp"), P("ctx", "tp"), P("ctx", "tp"), P("ctx", "tp"), P())
    out_specs = (P("ctx", "tp"), P("ctx", "tp"), P("ctx", "tp"), P("ctx", "tp"))
    return jax.shard_map(
        functools.partial(on_device, n_ctx=mesh.shape["ctx"]),
        mesh=mesh,
        in_specs=in_specs,
        out_specs=out_specs,
        check_vma=False,
    )
```

```python
import functools
import math

import jax
import jax.numpy as jnp
from jax import lax
from jax.experimental import pallas as pl
from jax.experimental.pallas import tpu as pltpu
from jax.sharding import PartitionSpec as P

HD = 128
BLK = 256
NEG_FILL = -1e30
MESH = pl.DeviceIdType.MESH


def dot(a, b):
    return jnp.dot(a, b, preferred_element_type=jnp.float32)


def kernel(
    n_ctx,
    tokens,
    share,
    doc_ref,
    q_hbm,
    kt_hbm,
    vt_hbm,
    do_hbm,
    out_ref,
    dq_ref,
    dkt_ref,
    dvt_ref,
    q_ref,
    do_ref,
    qt_ref,
    dot_ref,
    kv_ref,
    k_ref,
    v_ref,
    start_ref,
    s_ref,
    p_ref,
    delta_ref,
    max_ref,
    inv_ref,
    ret_send,
    ret_recv,
    total_ref,
    rs_send,
    rs_recv,
    load_sem,
    g_send,
    g_recv,
    f_send,
    f_recv,
    b_send,
    b_recv,
    r_send,
    r_recv,
):
    scale = 1.0 / math.sqrt(HD)
    factor = scale * math.log2(math.e)
    ctx = lax.axis_index("ctx")
    tp = lax.axis_index("tp")
    place = lax.rem(tp, share)
    base = tp - place
    band = HD // share
    nxt = lax.rem(ctx + 1, n_ctx)
    prv = lax.rem(ctx + n_ctx - 1, n_ctx)
    span = tokens + BLK
    blocks = tokens // BLK
    own = pl.ds(tokens, tokens)
    before = pl.ds(0, tokens)
    kv_hbm = (kt_hbm, vt_hbm)

    def other(d):
        return lax.rem(place + d, share)

    def band_of(index):
        return pl.ds(pl.multiple_of(index * band, band), band)

    load_q = pltpu.make_async_copy(q_hbm, q_ref, load_sem.at[0])
    load_do = pltpu.make_async_copy(do_hbm, do_ref, load_sem.at[1])
    load_kv = [
        pltpu.make_async_copy(
            kv_hbm[i], kv_ref.at[i, band_of(place), own], load_sem.at[2 + i]
        )
        for i in range(2)
    ]
    for c in [load_q, load_do] + load_kv:
        c.start()

    barrier = pltpu.get_barrier_semaphore()
    for d in range(1, share):
        pl.semaphore_signal(
            barrier, inc=1, device_id=(ctx, base + other(d)), device_id_type=MESH
        )
    for c in (nxt, prv):
        pl.semaphore_signal(barrier, inc=1, device_id=(c, tp), device_id_type=MESH)
    pl.semaphore_wait(barrier, share + 1)

    def gather(i):
        copies = [
            pltpu.make_async_remote_copy(
                src_ref=kv_hbm[i],
                dst_ref=kv_ref.at[i, band_of(place), own],
                send_sem=g_send.at[i, d - 1],
                recv_sem=g_recv.at[i, d - 1],
                device_id=(ctx, base + other(d)),
                device_id_type=MESH,
            )
            for d in range(1, share)
        ]
        return copies

    def forward(i, d):
        which = lax.rem(place - d + share, share)
        src = kv_hbm[i] if d == 0 else kv_ref.at[i, band_of(which), own]
        return pltpu.make_async_remote_copy(
            src_ref=src,
            dst_ref=kv_ref.at[i, band_of(which), before],
            send_sem=f_send.at[i, d],
            recv_sem=f_recv.at[i, d],
            device_id=(nxt, tp),
            device_id_type=MESH,
        )

    gathers = [gather(i) for i in range(2)]
    forwards = [[forward(i, d) for d in range(share)] for i in range(2)]

    for c in gathers[0]:
        c.start()
    forwards[0][0].start()

    row_base = ctx * tokens
    window_base = row_base - tokens

    ends = []
    running = doc_ref[0]
    for k in range(1, doc_ref.shape[0]):
        ends.append(running)
        running = running + doc_ref[k]
    lane = lax.broadcasted_iota(jnp.int32, (128, 128), 1)
    sub = lax.broadcasted_iota(jnp.int32, (128, 128), 0)

    def find_start(chunk, carry):
        pos = sub + (row_base + chunk * 128)
        first = jnp.zeros((128, 128), jnp.int32)
        for e in ends:
            first = jnp.where(pos >= e, e, first)
        rows = pl.ds(pl.multiple_of(chunk * 128, 128), 128)
        start_ref[rows, :] = first - window_base - lane
        return carry

    lax.fori_loop(0, tokens // 128, find_start, 0)
    load_q.wait()
    load_do.wait()

    for c in gathers[0]:
        c.wait_send()
    for c in gathers[1]:
        c.start()
    forwards[1][0].start()
    load_kv[0].wait()
    for d in range(1, share):
        gathers[0][d - 1].wait_recv()
        forwards[0][d].start()

    lane32 = lax.broadcasted_iota(jnp.int32, (32, 128), 1)
    sub32 = lax.broadcasted_iota(jnp.int32, (32, 128), 0)

    def heads_of(ref, rows):
        return jnp.concatenate([ref[rows, 0:HD], ref[rows, HD : 2 * HD]], axis=0)

    def middle(b):
        return tokens - b * BLK

    def score(b, first, last):
        rows, cols = slice(b * BLK, b * BLK + BLK), slice(b * BLK + first, b * BLK + last)
        s_ref[b, :, first:last] = dot(heads_of(q_ref, rows), kv_ref[0, :, cols])

    def masked(b, r, j, begin):
        low, first = r % BLK, j * 128 - tokens
        part = s_ref[b, r : r + 32, j * 128 : j * 128 + 128]
        ok = begin <= b * BLK + j * 128
        if first + 127 > low:
            ok = ok & (lane32 + first <= sub32 + low)
        return jnp.where(ok, part, NEG_FILL)

    def own_max(b):
        for r in range(0, 2 * BLK, 32):
            head, low = r // BLK, b * BLK + r % BLK
            begin = start_ref[low : low + 32, :]
            top = masked(b, r, middle(b) // 128, begin)
            for j in range(middle(b) // 128 + 1, span // 128):
                top = jnp.maximum(top, masked(b, r, j, begin))
            max_ref[head, low : low + 32, :] = top

    def row_max(b):
        for r in range(0, 2 * BLK, 32):
            head, low = r // BLK, b * BLK + r % BLK
            begin = start_ref[low : low + 32, :]
            top = max_ref[head, low : low + 32, :]
            for j in range(middle(b) // 128):
                top = jnp.maximum(top, masked(b, r, j, begin))
            top = jnp.max(top, axis=1, keepdims=True)
            max_ref[head, low : low + 32, :] = jnp.broadcast_to(top, (32, 128))

    def probabilities(b):
        for r in range(0, 2 * BLK, 32):
            head, low = r // BLK, b * BLK + r % BLK
            begin = start_ref[low : low + 32, :]
            top = max_ref[head, low : low + 32, :]
            total = jnp.zeros((32, 128), jnp.float32)
            for j in range(span // 128):
                prob = jnp.exp2((masked(b, r, j, begin) - top) * factor)
                total = total + prob
                cols = slice(b * BLK + j * 128, b * BLK + j * 128 + 128)
                p_ref[head, low : low + 32, cols] = prob.astype(jnp.bfloat16)
            inverse = 1.0 / jnp.sum(total, axis=1, keepdims=True)
            inv_ref[head, low : low + 32, :] = jnp.broadcast_to(inverse, (32, 128))

    def scaled_turned(src_ref, dst_ref, b):
        rows = slice(b * BLK, b * BLK + BLK)
        for h in range(2):
            cols = slice(h * HD, h * HD + HD)
            part = src_ref[rows, cols].astype(jnp.float32) * inv_ref[h, rows, :]
            dst_ref[cols, rows] = part.astype(jnp.bfloat16).T

    left = (qt_ref, dot_ref)
    weights = (scale, 1.0)

    def rows_of(kc):
        return range(max(0, kc - blocks), min(blocks - 1, kc) + 1)

    def column_sum(i, kc):
        rows = slice(rows_of(kc)[0] * BLK, rows_of(kc)[-1] * BLK + BLK)
        cols = slice(kc * BLK, (kc + 1) * BLK)
        total = dot(left[i][0:HD, rows], p_ref[0, rows, cols]) + dot(
            left[i][HD : 2 * HD, rows], p_ref[1, rows, cols]
        )
        return total * weights[i] if weights[i] != 1.0 else total

    def back(i, kc):
        cols = pl.ds(kc * BLK, BLK)
        return pltpu.make_async_remote_copy(
            src_ref=ret_send.at[i, :, cols],
            dst_ref=ret_recv.at[i, :, cols],
            send_sem=b_send.at[i, kc],
            recv_sem=b_recv.at[i, kc],
            device_id=(prv, tp),
            device_id_type=MESH,
        )

    pieces = ((1,) * blocks, (blocks // 2,) * 2)

    def scatter(i, piece, d):
        size = pieces[i][piece] * BLK
        cols = pl.ds(sum(pieces[i][:piece]) * BLK, size)
        return pltpu.make_async_remote_copy(
            src_ref=rs_send.at[i, band_of(other(d)), cols],
            dst_ref=rs_recv.at[i, d - 1, :, cols],
            send_sem=r_send.at[i, piece, d - 1],
            recv_sem=r_recv.at[i, piece, d - 1],
            device_id=(ctx, base + other(d)),
            device_id_type=MESH,
        )

    backs = [[back(i, kc) for kc in range(blocks)] for i in range(2)]
    scatters = [
        [[scatter(i, piece, d) for d in range(1, share)] for piece in range(len(pieces[i]))]
        for i in range(2)
    ]

    def column_back(i, kc):
        ret_send[i, :, kc * BLK : (kc + 1) * BLK] = column_sum(i, kc).astype(jnp.bfloat16)

    def add_returned(i, kc, mine):
        cols = slice(kc * BLK, (kc + 1) * BLK)
        backs[i][kc].wait_recv()
        total = mine + ret_recv[i, :, cols].astype(jnp.float32)
        total_ref[i, :, cols] = total
        rs_send[i, :, cols] = total.astype(jnp.bfloat16)

    def finish(i):
        for piece in scatters[i]:
            for c in piece:
                c.wait_recv()
        result = total_ref[i, band_of(place), :]
        for d in range(1, share):
            result = result + rs_recv[i, d - 1].astype(jnp.float32)
        (dkt_ref, dvt_ref)[i][...] = result.astype(jnp.bfloat16)

    score(0, middle(0), span)
    for b in range(blocks):
        if b + 1 < blocks:
            score(b + 1, middle(b + 1), span)
        own_max(b)
    for d in range(share):
        forwards[0][d].wait_recv()

    score(0, 0, middle(0))
    row_max(0)
    score(1, 0, middle(1))
    for b in range(blocks):
        if b + 2 < blocks:
            score(b + 2, 0, middle(b + 2))
        if b + 1 < blocks:
            row_max(b + 1)
        if b:
            column_back(1, b - 1)
        probabilities(b)
        scaled_turned(do_ref, dot_ref, b)
        if b:
            backs[1][b - 1].start()
        if b == 2:
            for d in range(1, share):
                gathers[1][d - 1].wait_recv()
                forwards[1][d].start()
            load_kv[1].wait()

    column_back(1, blocks - 1)
    backs[1][blocks - 1].start()
    for kc in range(blocks):
        total_ref[1, :, kc * BLK : (kc + 1) * BLK] = column_sum(1, kc + blocks)
    for b in range(blocks):
        scaled_turned(q_ref, qt_ref, b)
    v_ref[own, :] = kv_ref[1, :, own].T
    for d in range(share):
        forwards[1][d].wait_recv()
    v_ref[before, :] = kv_ref[1, :, before].T

    def outputs(b):
        rows, window = slice(b * BLK, b * BLK + BLK), slice(b * BLK, b * BLK + span)
        prob = jnp.concatenate([p_ref[0, rows, window], p_ref[1, rows, window]], axis=0)
        sums = dot(prob, v_ref[window, :])
        for h in range(2):
            part = (sums[h * BLK : h * BLK + BLK] * inv_ref[h, rows, :]).astype(jnp.bfloat16)
            out_ref[rows, h * HD : h * HD + HD] = part
            grads = do_ref[rows, h * HD : h * HD + HD].astype(jnp.float32)
            delta = jnp.sum(grads * part.astype(jnp.float32), axis=1, keepdims=True)
            delta_ref[h, rows, :] = jnp.broadcast_to(delta, (BLK, 128))

    for b in range(blocks):
        outputs(b)
        if b == 0:
            for kc in range(blocks):
                add_returned(1, kc, total_ref[1, :, kc * BLK : (kc + 1) * BLK])
                if kc % 2:
                    for c in scatters[1][kc // 2]:
                        c.start()

    def score_grads(b, kc):
        rows, cols = slice(b * BLK, b * BLK + BLK), slice(kc * BLK, kc * BLK + BLK)
        change = dot(heads_of(do_ref, rows), kv_ref[1, :, cols])
        for r in range(0, 2 * BLK, 64):
            head, low = r // BLK, r % BLK
            these = slice(b * BLK + low, b * BLK + low + 64)
            delta = delta_ref[head, these, :]
            delta = jnp.concatenate([delta] * (BLK // 128), axis=1)
            held = p_ref[head, these, cols].astype(jnp.float32)
            p_ref[head, these, cols] = (held * (change[r : r + 64] - delta)).astype(jnp.bfloat16)

    for b in rows_of(0):
        score_grads(b, 0)
    for kc in range(2 * blocks):
        if kc + 1 < 2 * blocks:
            for b in rows_of(kc + 1):
                score_grads(b, kc + 1)
        if kc < blocks:
            column_back(0, kc)
            backs[0][kc].start()
        else:
            add_returned(0, kc - blocks, column_sum(0, kc))
            for c in scatters[0][kc - blocks]:
                c.start()

    k_ref[...] = kv_ref[0].T
    finish(1)

    for b in range(blocks):
        rows, window = slice(b * BLK, b * BLK + BLK), slice(b * BLK, b * BLK + span)
        dscore = jnp.concatenate([p_ref[0, rows, window], p_ref[1, rows, window]], axis=0)
        sums = dot(dscore, k_ref[window, :])
        for h in range(2):
            part = sums[h * BLK : h * BLK + BLK] * (inv_ref[h, rows, :] * scale)
            dq_ref[rows, h * HD : h * HD + HD] = part.astype(jnp.bfloat16)

    finish(0)

    for i in range(2):
        for c in (gathers[i] if i else []) + forwards[i] + backs[i] + sum(scatters[i], []):
            c.wait_send()


def hand_over(*refs):
    count = len(refs) // 2
    sems = refs[-1]
    copies = [
        pltpu.make_async_copy(refs[i], refs[count + i], sems.at[i]) for i in range(count)
    ]
    for c in copies:
        c.start()
    for c in copies:
        c.wait()


def on_device(queries, keys, values, grad_out, doc_lengths, *, n_ctx):
    tokens, width = queries.shape
    columns = keys.shape[1]
    share = HD // columns
    blocks = tokens // BLK
    bf16, f32 = jnp.bfloat16, jnp.float32
    anywhere = pl.BlockSpec(memory_space=pltpu.HBM)
    dma = pltpu.SemaphoreType.DMA
    shapes = [(tokens, width), (tokens, width), (columns, tokens), (columns, tokens)]
    results = pl.pallas_call(
        functools.partial(kernel, n_ctx, tokens, share),
        out_shape=[pltpu.VMEM(shape, bf16) for shape in shapes],
        in_specs=[pl.BlockSpec(memory_space=pltpu.SMEM)] + [anywhere] * 4,
        out_specs=[pl.BlockSpec(memory_space=pltpu.VMEM)] * 4,
        scratch_shapes=[
            pltpu.VMEM((tokens, width), bf16),
            pltpu.VMEM((tokens, width), bf16),
            pltpu.VMEM((width, tokens), bf16),
            pltpu.VMEM((width, tokens), bf16),
            pltpu.VMEM((2, HD, 2 * tokens), bf16),
            pltpu.VMEM((2 * tokens, HD), bf16),
            pltpu.VMEM((2 * tokens, HD), bf16),
            pltpu.VMEM((tokens, 128), jnp.int32),
            pltpu.VMEM((blocks, 2 * BLK, tokens + BLK), f32),
            pltpu.VMEM((2, tokens, 2 * tokens), bf16),
            pltpu.VMEM((2, tokens, 128), f32),
            pltpu.VMEM((2, tokens, 128), f32),
            pltpu.VMEM((2, tokens, 128), f32),
            pltpu.VMEM((2, HD, tokens), bf16),
            pltpu.VMEM((2, HD, tokens), bf16),
            pltpu.VMEM((2, HD, tokens), f32),
            pltpu.VMEM((2, HD, tokens), bf16),
            pltpu.VMEM((2, share - 1, columns, tokens), bf16),
            dma((4,)),
            dma((2, share - 1)),
            dma((2, share - 1)),
            dma((2, share)),
            dma((2, share)),
            dma((2, blocks)),
            dma((2, blocks)),
            dma((2, blocks, share - 1)),
            dma((2, blocks, share - 1)),
        ],
        compiler_params=pltpu.CompilerParams(
            collective_id=0, has_side_effects=True, vmem_limit_bytes=60 * 1024 * 1024
        ),
        cost_estimate=pl.CostEstimate(
            flops=6 * 2 * 2 * tokens * (tokens + BLK) * HD,
            bytes_accessed=4 * tokens * width * 2,
            transcendentals=2 * tokens * (tokens + BLK),
        ),
    )(doc_lengths, queries, keys.T, values.T, grad_out)
    out, dq, dkt, dvt = pl.pallas_call(
        hand_over,
        out_shape=[jax.ShapeDtypeStruct(shape, bf16) for shape in shapes],
        in_specs=[pl.BlockSpec(memory_space=pltpu.VMEM)] * 4,
        out_specs=[anywhere] * 4,
        scratch_shapes=[dma((4,))],
        compiler_params=pltpu.CompilerParams(vmem_limit_bytes=4 * 1024 * 1024),
        cost_estimate=pl.CostEstimate(
            flops=0, bytes_accessed=2 * tokens * width * 2, transcendentals=0
        ),
    )(*results)
    return out, dq, dkt.T, dvt.T


def solution(mesh):
    in_specs = (P("ctx", "tp"), P("ctx", "tp"), P("ctx", "tp"), P("ctx", "tp"), P())
    out_specs = (P("ctx", "tp"), P("ctx", "tp"), P("ctx", "tp"), P("ctx", "tp"))
    return jax.shard_map(
        functools.partial(on_device, n_ctx=mesh.shape["ctx"]),
        mesh=mesh,
        in_specs=in_specs,
        out_specs=out_specs,
        check_vma=False,
    )
```

```python
import functools
import math

import jax
import jax.numpy as jnp
from jax import lax
from jax.experimental import pallas as pl
from jax.experimental.pallas import tpu as pltpu
from jax.sharding import PartitionSpec as P

HD = 128
BLK = 256
NEG_FILL = -1e30
MESH = pl.DeviceIdType.MESH


def dot(a, b):
    return jnp.dot(a, b, preferred_element_type=jnp.float32)


def kernel(
    n_ctx,
    tokens,
    share,
    doc_ref,
    q_hbm,
    kt_hbm,
    vt_hbm,
    do_hbm,
    out_ref,
    dq_ref,
    dkt_ref,
    dvt_ref,
    q_ref,
    do_ref,
    qt_ref,
    dot_ref,
    kv_ref,
    k_ref,
    v_ref,
    bias_ref,
    s_ref,
    p_ref,
    delta_ref,
    max_ref,
    inv_ref,
    ret_send,
    ret_recv,
    total_ref,
    rs_send,
    rs_recv,
    load_sem,
    g_send,
    g_recv,
    f_send,
    f_recv,
    b_send,
    b_recv,
    r_send,
    r_recv,
):
    scale = 1.0 / math.sqrt(HD)
    factor = scale * math.log2(math.e)
    ctx = lax.axis_index("ctx")
    tp = lax.axis_index("tp")
    place = lax.rem(tp, share)
    base = tp - place
    band = HD // share
    nxt = lax.rem(ctx + 1, n_ctx)
    prv = lax.rem(ctx + n_ctx - 1, n_ctx)
    span = tokens + BLK
    blocks = tokens // BLK
    own = pl.ds(tokens, tokens)
    before = pl.ds(0, tokens)
    kv_hbm = (kt_hbm, vt_hbm)

    def other(d):
        return lax.rem(place + d, share)

    def band_of(index):
        return pl.ds(pl.multiple_of(index * band, band), band)

    load_q = pltpu.make_async_copy(q_hbm, q_ref, load_sem.at[0])
    load_do = pltpu.make_async_copy(do_hbm, do_ref, load_sem.at[1])
    load_kv = [
        pltpu.make_async_copy(
            kv_hbm[i], kv_ref.at[i, band_of(place), own], load_sem.at[2 + i]
        )
        for i in range(2)
    ]
    for c in [load_q, load_do] + load_kv:
        c.start()

    barrier = pltpu.get_barrier_semaphore()
    for d in range(1, share):
        pl.semaphore_signal(
            barrier, inc=1, device_id=(ctx, base + other(d)), device_id_type=MESH
        )
    for c in (nxt, prv):
        pl.semaphore_signal(barrier, inc=1, device_id=(c, tp), device_id_type=MESH)
    pl.semaphore_wait(barrier, share + 1)

    def gather(i):
        copies = [
            pltpu.make_async_remote_copy(
                src_ref=kv_hbm[i],
                dst_ref=kv_ref.at[i, band_of(place), own],
                send_sem=g_send.at[i, d - 1],
                recv_sem=g_recv.at[i, d - 1],
                device_id=(ctx, base + other(d)),
                device_id_type=MESH,
            )
            for d in range(1, share)
        ]
        return copies

    def forward(i, d):
        which = lax.rem(place - d + share, share)
        src = kv_hbm[i] if d == 0 else kv_ref.at[i, band_of(which), own]
        return pltpu.make_async_remote_copy(
            src_ref=src,
            dst_ref=kv_ref.at[i, band_of(which), before],
            send_sem=f_send.at[i, d],
            recv_sem=f_recv.at[i, d],
            device_id=(nxt, tp),
            device_id_type=MESH,
        )

    gathers = [gather(i) for i in range(2)]
    forwards = [[forward(i, d) for d in range(share)] for i in range(2)]

    for c in gathers[0]:
        c.start()
    forwards[0][0].start()

    row_base = ctx * tokens
    window_base = row_base - tokens

    ends = []
    running = doc_ref[0]
    for k in range(1, doc_ref.shape[0]):
        ends.append(running)
        running = running + doc_ref[k]
    lane = lax.broadcasted_iota(jnp.int32, (128, 128), 1)
    sub = lax.broadcasted_iota(jnp.int32, (128, 128), 0)

    def find_start(chunk, carry):
        pos = sub + (row_base + chunk * 128)
        first = jnp.zeros((128, 128), jnp.int32)
        for e in ends:
            first = jnp.where(pos >= e, e, first)
        rows = pl.ds(pl.multiple_of(chunk * 128, 128), 128)
        turn = lax.rem(chunk, BLK // 128) * 128
        begin = first - window_base - lane - (chunk * 128 - turn)
        for j in range(span // 128):
            ok = begin <= j * 128
            if j * 128 >= tokens:
                ok = ok & (lane + (j * 128 - tokens) <= sub + turn)
            bias_ref[rows, j * 128 : j * 128 + 128] = jnp.where(ok, 0.0, NEG_FILL)
        return carry

    lax.fori_loop(0, tokens // 128, find_start, 0)
    load_q.wait()
    load_do.wait()

    for c in gathers[0]:
        c.wait_send()
    for c in gathers[1]:
        c.start()
    forwards[1][0].start()
    load_kv[0].wait()
    for d in range(1, share):
        gathers[0][d - 1].wait_recv()
        forwards[0][d].start()

    def heads_of(ref, rows):
        return jnp.concatenate([ref[rows, 0:HD], ref[rows, HD : 2 * HD]], axis=0)

    def middle(b):
        return tokens - b * BLK

    def scores(b, first, last):
        def piece(col):
            rows = slice(b * BLK, b * BLK + BLK)
            cols = slice(b * BLK + col, b * BLK + col + BLK)
            bias = bias_ref[rows, col : col + BLK]
            part = dot(heads_of(q_ref, rows), kv_ref[0, :, cols])
            s_ref[b, 0:BLK, col : col + BLK] = part[0:BLK] + bias
            s_ref[b, BLK : 2 * BLK, col : col + BLK] = part[BLK : 2 * BLK] + bias

        return [functools.partial(piece, col) for col in range(first, last, BLK)]

    def own_max(b):
        def piece(r):
            head, low = r // BLK, b * BLK + r % BLK
            first = middle(b) // 128
            top = s_ref[b, r : r + 32, first * 128 : first * 128 + 128]
            for j in range(first + 1, span // 128):
                top = jnp.maximum(top, s_ref[b, r : r + 32, j * 128 : j * 128 + 128])
            max_ref[head, low : low + 32, :] = top

        return [functools.partial(piece, r) for r in range(0, 2 * BLK, 32)]

    def row_max(b):
        def piece(r):
            head, low = r // BLK, b * BLK + r % BLK
            top = max_ref[head, low : low + 32, :]
            for j in range(middle(b) // 128):
                top = jnp.maximum(top, s_ref[b, r : r + 32, j * 128 : j * 128 + 128])
            top = jnp.max(top, axis=1, keepdims=True)
            max_ref[head, low : low + 32, :] = jnp.broadcast_to(top, (32, 128))

        return [functools.partial(piece, r) for r in range(0, 2 * BLK, 32)]

    def probabilities(b):
        def piece(r):
            head, low = r // BLK, b * BLK + r % BLK
            top = max_ref[head, low : low + 32, :]
            total = jnp.zeros((32, 128), jnp.float32)
            for j in range(span // 128):
                part = s_ref[b, r : r + 32, j * 128 : j * 128 + 128]
                prob = jnp.exp2((part - top) * factor)
                total = total + prob
                cols = slice(b * BLK + j * 128, b * BLK + j * 128 + 128)
                p_ref[head, low : low + 32, cols] = prob.astype(jnp.bfloat16)
            inverse = 1.0 / jnp.sum(total, axis=1, keepdims=True)
            inv_ref[head, low : low + 32, :] = jnp.broadcast_to(inverse, (32, 128))

        return [functools.partial(piece, r) for r in range(0, 2 * BLK, 32)]

    def weave(*lists):
        order = [
            ((n + 0.5) / len(pieces_of), k, piece)
            for k, pieces_of in enumerate(lists)
            for n, piece in enumerate(pieces_of)
        ]
        for _, _, piece in sorted(order, key=lambda entry: entry[:2]):
            piece()

    def scaled_turned(src_ref, dst_ref, b):
        rows = slice(b * BLK, b * BLK + BLK)
        for h in range(2):
            cols = slice(h * HD, h * HD + HD)
            part = src_ref[rows, cols].astype(jnp.float32) * inv_ref[h, rows, :]
            dst_ref[cols, rows] = part.astype(jnp.bfloat16).T

    left = (qt_ref, dot_ref)
    weights = (scale, 1.0)

    def rows_of(kc):
        return range(max(0, kc - blocks), min(blocks - 1, kc) + 1)

    def column_sum(i, kc):
        rows = slice(rows_of(kc)[0] * BLK, rows_of(kc)[-1] * BLK + BLK)
        cols = slice(kc * BLK, (kc + 1) * BLK)
        total = dot(left[i][0:HD, rows], p_ref[0, rows, cols]) + dot(
            left[i][HD : 2 * HD, rows], p_ref[1, rows, cols]
        )
        return total * weights[i] if weights[i] != 1.0 else total

    def back(i, kc):
        cols = pl.ds(kc * BLK, BLK)
        return pltpu.make_async_remote_copy(
            src_ref=ret_send.at[i, :, cols],
            dst_ref=ret_recv.at[i, :, cols],
            send_sem=b_send.at[i, kc],
            recv_sem=b_recv.at[i, kc],
            device_id=(prv, tp),
            device_id_type=MESH,
        )

    pieces = ((1,) * blocks, (blocks // 2,) * 2)

    def scatter(i, piece, d):
        size = pieces[i][piece] * BLK
        cols = pl.ds(sum(pieces[i][:piece]) * BLK, size)
        return pltpu.make_async_remote_copy(
            src_ref=rs_send.at[i, band_of(other(d)), cols],
            dst_ref=rs_recv.at[i, d - 1, :, cols],
            send_sem=r_send.at[i, piece, d - 1],
            recv_sem=r_recv.at[i, piece, d - 1],
            device_id=(ctx, base + other(d)),
            device_id_type=MESH,
        )

    backs = [[back(i, kc) for kc in range(blocks)] for i in range(2)]
    scatters = [
        [[scatter(i, piece, d) for d in range(1, share)] for piece in range(len(pieces[i]))]
        for i in range(2)
    ]

    def column_back(i, kc):
        ret_send[i, :, kc * BLK : (kc + 1) * BLK] = column_sum(i, kc).astype(jnp.bfloat16)

    def add_returned(i, kc, mine):
        cols = slice(kc * BLK, (kc + 1) * BLK)
        backs[i][kc].wait_recv()
        total = mine + ret_recv[i, :, cols].astype(jnp.float32)
        total_ref[i, :, cols] = total
        rs_send[i, :, cols] = total.astype(jnp.bfloat16)

    def finish(i):
        for piece in scatters[i]:
            for c in piece:
                c.wait_recv()
        result = total_ref[i, band_of(place), :]
        for d in range(1, share):
            result = result + rs_recv[i, d - 1].astype(jnp.float32)
        (dkt_ref, dvt_ref)[i][...] = result.astype(jnp.bfloat16)

    weave(scores(0, middle(0), span))
    for b in range(blocks):
        ahead = scores(b + 1, middle(b + 1), span) if b + 1 < blocks else []
        weave(ahead, own_max(b))
    for d in range(share):
        forwards[0][d].wait_recv()

    weave(scores(0, 0, middle(0)))
    weave(scores(1, 0, middle(1)), row_max(0))
    for b in range(blocks):
        matrix, vector = [], []
        if b:
            matrix.append(functools.partial(column_back, 1, b - 1))
        if b + 2 < blocks:
            matrix += scores(b + 2, 0, middle(b + 2))
        if b + 1 < blocks:
            vector = row_max(b + 1)
        weave(matrix, vector, probabilities(b))
        scaled_turned(do_ref, dot_ref, b)
        if b:
            backs[1][b - 1].start()
        if b == 2:
            for d in range(1, share):
                gathers[1][d - 1].wait_recv()
                forwards[1][d].start()
            load_kv[1].wait()

    column_back(1, blocks - 1)
    backs[1][blocks - 1].start()
    for kc in range(blocks):
        total_ref[1, :, kc * BLK : (kc + 1) * BLK] = column_sum(1, kc + blocks)
    for b in range(blocks):
        scaled_turned(q_ref, qt_ref, b)
    v_ref[own, :] = kv_ref[1, :, own].T
    for d in range(share):
        forwards[1][d].wait_recv()
    v_ref[before, :] = kv_ref[1, :, before].T

    def outputs(b):
        rows, window = slice(b * BLK, b * BLK + BLK), slice(b * BLK, b * BLK + span)
        prob = jnp.concatenate([p_ref[0, rows, window], p_ref[1, rows, window]], axis=0)
        sums = dot(prob, v_ref[window, :])
        for h in range(2):
            part = (sums[h * BLK : h * BLK + BLK] * inv_ref[h, rows, :]).astype(jnp.bfloat16)
            out_ref[rows, h * HD : h * HD + HD] = part
            grads = do_ref[rows, h * HD : h * HD + HD].astype(jnp.float32)
            delta = jnp.sum(grads * part.astype(jnp.float32), axis=1, keepdims=True)
            delta_ref[h, rows, :] = jnp.broadcast_to(delta, (BLK, 128))

    def tile_change(b, kc):
        rows, cols = slice(b * BLK, b * BLK + BLK), slice(kc * BLK, kc * BLK + BLK)
        return dot(heads_of(do_ref, rows), kv_ref[1, :, cols])

    def tile_scores(b, kc, change):
        def piece(r):
            cols = slice(kc * BLK, kc * BLK + BLK)
            head, low = r // BLK, r % BLK
            these = slice(b * BLK + low, b * BLK + low + 64)
            delta = delta_ref[head, these, :]
            delta = jnp.concatenate([delta] * (BLK // 128), axis=1)
            held = p_ref[head, these, cols].astype(jnp.float32)
            p_ref[head, these, cols] = (held * (change[r : r + 64] - delta)).astype(jnp.bfloat16)

        return [functools.partial(piece, r) for r in range(0, 2 * BLK, 64)]

    def query_grads(b):
        rows, window = slice(b * BLK, b * BLK + BLK), slice(b * BLK, b * BLK + span)
        dscore = jnp.concatenate([p_ref[0, rows, window], p_ref[1, rows, window]], axis=0)
        sums = dot(dscore, k_ref[window, :])
        for h in range(2):
            part = sums[h * BLK : h * BLK + BLK] * (inv_ref[h, rows, :] * scale)
            dq_ref[rows, h * HD : h * HD + HD] = part.astype(jnp.bfloat16)

    outputs(0)
    for kc in range(blocks):
        add_returned(1, kc, total_ref[1, :, kc * BLK : (kc + 1) * BLK])
        if kc % 2:
            for c in scatters[1][kc // 2]:
                c.start()

    tiles = [(b, kc) for kc in range(2 * blocks) for b in rows_of(kc)]
    change = tile_change(*tiles[0])
    column = [None]
    ready = []
    for number, (b, kc) in enumerate(tiles):
        following = [None]
        matrix = []
        if number + 1 < len(tiles):

            def ahead(number=number, following=following):
                following[0] = tile_change(*tiles[number + 1])

            matrix.append(ahead)
        if ready:
            which = ready[0]

            def total(which=which):
                if which < blocks:
                    column_back(0, which)
                else:
                    column[0] = column_sum(0, which)

            matrix.append(total)
            if which < blocks - 1:
                matrix.append(functools.partial(outputs, which + 2)) if which + 2 < blocks else None
        if number == 0:
            matrix.append(functools.partial(outputs, 1))
        weave(matrix, tile_scores(b, kc, change))
        change = following[0]
        if ready:
            which = ready.pop()
            if which < blocks:
                backs[0][which].start()
            else:
                add_returned(0, which - blocks, column[0])
                for c in scatters[0][which - blocks]:
                    c.start()
            if which == blocks - 1:
                k_ref[...] = kv_ref[0].T
            if which in (blocks, blocks + 1):
                query_grads(which - blocks)
        if b == rows_of(kc)[-1]:
            ready.append(kc)
    add_returned(0, blocks - 1, column_sum(0, 2 * blocks - 1))
    for c in scatters[0][blocks - 1]:
        c.start()

    finish(1)

    for b in range(2, blocks):
        query_grads(b)

    finish(0)

    for i in range(2):
        for c in (gathers[i] if i else []) + forwards[i] + backs[i] + sum(scatters[i], []):
            c.wait_send()


def hand_over(*refs):
    count = len(refs) // 2
    sems = refs[-1]
    copies = [
        pltpu.make_async_copy(refs[i], refs[count + i], sems.at[i]) for i in range(count)
    ]
    for c in copies:
        c.start()
    for c in copies:
        c.wait()


def on_device(queries, keys, values, grad_out, doc_lengths, *, n_ctx):
    tokens, width = queries.shape
    columns = keys.shape[1]
    share = HD // columns
    blocks = tokens // BLK
    bf16, f32 = jnp.bfloat16, jnp.float32
    anywhere = pl.BlockSpec(memory_space=pltpu.HBM)
    dma = pltpu.SemaphoreType.DMA
    shapes = [(tokens, width), (tokens, width), (columns, tokens), (columns, tokens)]
    results = pl.pallas_call(
        functools.partial(kernel, n_ctx, tokens, share),
        out_shape=[pltpu.VMEM(shape, bf16) for shape in shapes],
        in_specs=[pl.BlockSpec(memory_space=pltpu.SMEM)] + [anywhere] * 4,
        out_specs=[pl.BlockSpec(memory_space=pltpu.VMEM)] * 4,
        scratch_shapes=[
            pltpu.VMEM((tokens, width), bf16),
            pltpu.VMEM((tokens, width), bf16),
            pltpu.VMEM((width, tokens), bf16),
            pltpu.VMEM((width, tokens), bf16),
            pltpu.VMEM((2, HD, 2 * tokens), bf16),
            pltpu.VMEM((2 * tokens, HD), bf16),
            pltpu.VMEM((2 * tokens, HD), bf16),
            pltpu.VMEM((tokens, tokens + BLK), f32),
            pltpu.VMEM((blocks, 2 * BLK, tokens + BLK), f32),
            pltpu.VMEM((2, tokens, 2 * tokens), bf16),
            pltpu.VMEM((2, tokens, 128), f32),
            pltpu.VMEM((2, tokens, 128), f32),
            pltpu.VMEM((2, tokens, 128), f32),
            pltpu.VMEM((2, HD, tokens), bf16),
            pltpu.VMEM((2, HD, tokens), bf16),
            pltpu.VMEM((2, HD, tokens), f32),
            pltpu.VMEM((2, HD, tokens), bf16),
            pltpu.VMEM((2, share - 1, columns, tokens), bf16),
            dma((4,)),
            dma((2, share - 1)),
            dma((2, share - 1)),
            dma((2, share)),
            dma((2, share)),
            dma((2, blocks)),
            dma((2, blocks)),
            dma((2, blocks, share - 1)),
            dma((2, blocks, share - 1)),
        ],
        compiler_params=pltpu.CompilerParams(
            collective_id=0, has_side_effects=True, vmem_limit_bytes=60 * 1024 * 1024
        ),
        cost_estimate=pl.CostEstimate(
            flops=6 * 2 * 2 * tokens * (tokens + BLK) * HD,
            bytes_accessed=4 * tokens * width * 2,
            transcendentals=2 * tokens * (tokens + BLK),
        ),
    )(doc_lengths, queries, keys.T, values.T, grad_out)
    out, dq, dkt, dvt = pl.pallas_call(
        hand_over,
        out_shape=[jax.ShapeDtypeStruct(shape, bf16) for shape in shapes],
        in_specs=[pl.BlockSpec(memory_space=pltpu.VMEM)] * 4,
        out_specs=[anywhere] * 4,
        scratch_shapes=[dma((4,))],
        compiler_params=pltpu.CompilerParams(vmem_limit_bytes=4 * 1024 * 1024),
        cost_estimate=pl.CostEstimate(
            flops=0, bytes_accessed=2 * tokens * width * 2, transcendentals=0
        ),
    )(*results)
    return out, dq, dkt.T, dvt.T


def solution(mesh):
    in_specs = (P("ctx", "tp"), P("ctx", "tp"), P("ctx", "tp"), P("ctx", "tp"), P())
    out_specs = (P("ctx", "tp"), P("ctx", "tp"), P("ctx", "tp"), P("ctx", "tp"))
    return jax.shard_map(
        functools.partial(on_device, n_ctx=mesh.shape["ctx"]),
        mesh=mesh,
        in_specs=in_specs,
        out_specs=out_specs,
        check_vma=False,
    )
```

```python
import functools
import math

import jax
import jax.numpy as jnp
from jax import lax
from jax.experimental import pallas as pl
from jax.experimental.pallas import tpu as pltpu
from jax.sharding import PartitionSpec as P

HD = 128
BLK = 256
NEG_FILL = -1e30
MESH = pl.DeviceIdType.MESH


def dot(a, b):
    return jnp.dot(a, b, preferred_element_type=jnp.float32)


def kernel(
    n_ctx,
    tokens,
    share,
    doc_ref,
    q_hbm,
    kt_hbm,
    vt_hbm,
    do_hbm,
    out_ref,
    dq_ref,
    dkt_ref,
    dvt_ref,
    q_ref,
    do_ref,
    qt_ref,
    dot_ref,
    kv_ref,
    k_ref,
    v_ref,
    bias_ref,
    s_ref,
    p_ref,
    delta_ref,
    max_ref,
    inv_ref,
    ret_send,
    ret_recv,
    total_ref,
    rs_send,
    rs_recv,
    load_sem,
    g_send,
    g_recv,
    f_send,
    f_recv,
    b_send,
    b_recv,
    r_send,
    r_recv,
):
    scale = 1.0 / math.sqrt(HD)
    factor = scale * math.log2(math.e)
    ctx = lax.axis_index("ctx")
    tp = lax.axis_index("tp")
    place = lax.rem(tp, share)
    base = tp - place
    band = HD // share
    nxt = lax.rem(ctx + 1, n_ctx)
    prv = lax.rem(ctx + n_ctx - 1, n_ctx)
    span = tokens + BLK
    blocks = tokens // BLK
    own = pl.ds(tokens, tokens)
    before = pl.ds(0, tokens)
    kv_hbm = (kt_hbm, vt_hbm)

    in_middle = lax.rem((place + 1) // 2, 2) == 1
    at_an_end = jnp.logical_not(in_middle)
    others = (
        place,
        place + 1 - 2 * lax.rem(place, 2),
        place + 2 - 4 * (place // 2),
        share - 1 - place,
    )

    def other(d):
        return others[d]

    def band_of(index):
        return pl.ds(pl.multiple_of(index * band, band), band)

    load_q = pltpu.make_async_copy(q_hbm, q_ref, load_sem.at[0])
    load_do = pltpu.make_async_copy(do_hbm, do_ref, load_sem.at[1])
    load_kv = [
        pltpu.make_async_copy(
            kv_hbm[i], kv_ref.at[i, band_of(place), own], load_sem.at[2 + i]
        )
        for i in range(2)
    ]
    for c in [load_q, load_do] + load_kv:
        c.start()

    barrier = pltpu.get_barrier_semaphore()
    for d in range(1, share):
        pl.semaphore_signal(
            barrier, inc=1, device_id=(ctx, base + other(d)), device_id_type=MESH
        )
    for c in (nxt, prv):
        pl.semaphore_signal(barrier, inc=1, device_id=(c, tp), device_id_type=MESH)
    pl.semaphore_wait(barrier, share + 1)

    def gather(i):
        copies = [
            pltpu.make_async_remote_copy(
                src_ref=kv_hbm[i],
                dst_ref=kv_ref.at[i, band_of(place), own],
                send_sem=g_send.at[i, d - 1],
                recv_sem=g_recv.at[i, d - 1],
                device_id=(ctx, base + other(d)),
                device_id_type=MESH,
            )
            for d in range(1, share)
        ]
        return copies

    def forward(i, d):
        src = kv_hbm[i] if d == 0 else kv_ref.at[i, band_of(other(d)), own]
        return pltpu.make_async_remote_copy(
            src_ref=src,
            dst_ref=kv_ref.at[i, band_of(other(d)), before],
            send_sem=f_send.at[i, d],
            recv_sem=f_recv.at[i, d],
            device_id=(nxt, tp),
            device_id_type=MESH,
        )

    gathers = [gather(i) for i in range(2)]
    forwards = [[forward(i, d) for d in range(share)] for i in range(2)]

    for c in gathers[0]:
        c.start()
    forwards[0][0].start()

    row_base = ctx * tokens
    window_base = row_base - tokens

    ends = []
    running = doc_ref[0]
    for k in range(1, doc_ref.shape[0]):
        ends.append(running)
        running = running + doc_ref[k]
    lane = lax.broadcasted_iota(jnp.int32, (128, 128), 1)
    sub = lax.broadcasted_iota(jnp.int32, (128, 128), 0)

    def find_start(chunk, carry):
        pos = sub + (row_base + chunk * 128)
        first = jnp.zeros((128, 128), jnp.int32)
        for e in ends:
            first = jnp.where(pos >= e, e, first)
        rows = pl.ds(pl.multiple_of(chunk * 128, 128), 128)
        turn = lax.rem(chunk, BLK // 128) * 128
        begin = first - window_base - lane - (chunk * 128 - turn)
        for j in range(span // 128):
            ok = begin <= j * 128
            if j * 128 >= tokens:
                ok = ok & (lane + (j * 128 - tokens) <= sub + turn)
            bias_ref[rows, j * 128 : j * 128 + 128] = jnp.where(ok, 0.0, NEG_FILL)
        return carry

    lax.fori_loop(0, tokens // 128, find_start, 0)
    load_q.wait()
    load_do.wait()

    for c in gathers[0]:
        c.wait_send()
    for c in gathers[1]:
        c.start()
    forwards[1][0].start()
    load_kv[0].wait()
    for d in range(1, share):
        gathers[0][d - 1].wait_recv()
        forwards[0][d].start()

    def heads_of(ref, rows):
        return jnp.concatenate([ref[rows, 0:HD], ref[rows, HD : 2 * HD]], axis=0)

    def middle(b):
        return tokens - b * BLK

    def scores(b, first, last):
        def piece(col):
            rows = slice(b * BLK, b * BLK + BLK)
            cols = slice(b * BLK + col, b * BLK + col + BLK)
            bias = bias_ref[rows, col : col + BLK]
            part = dot(heads_of(q_ref, rows), kv_ref[0, :, cols])
            s_ref[b, 0:BLK, col : col + BLK] = part[0:BLK] + bias
            s_ref[b, BLK : 2 * BLK, col : col + BLK] = part[BLK : 2 * BLK] + bias

        return [functools.partial(piece, col) for col in range(first, last, BLK)]

    def own_max(b):
        def piece(r):
            head, low = r // BLK, b * BLK + r % BLK
            first = middle(b) // 128
            top = s_ref[b, r : r + 32, first * 128 : first * 128 + 128]
            for j in range(first + 1, span // 128):
                top = jnp.maximum(top, s_ref[b, r : r + 32, j * 128 : j * 128 + 128])
            max_ref[head, low : low + 32, :] = top

        return [functools.partial(piece, r) for r in range(0, 2 * BLK, 32)]

    def row_max(b):
        def piece(r):
            head, low = r // BLK, b * BLK + r % BLK
            top = max_ref[head, low : low + 32, :]
            for j in range(middle(b) // 128):
                top = jnp.maximum(top, s_ref[b, r : r + 32, j * 128 : j * 128 + 128])
            top = jnp.max(top, axis=1, keepdims=True)
            max_ref[head, low : low + 32, :] = jnp.broadcast_to(top, (32, 128))

        return [functools.partial(piece, r) for r in range(0, 2 * BLK, 32)]

    def probabilities(b):
        def piece(r):
            head, low = r // BLK, b * BLK + r % BLK
            top = max_ref[head, low : low + 32, :]
            total = jnp.zeros((32, 128), jnp.float32)
            for j in range(span // 128):
                part = s_ref[b, r : r + 32, j * 128 : j * 128 + 128]
                prob = jnp.exp2((part - top) * factor)
                total = total + prob
                cols = slice(b * BLK + j * 128, b * BLK + j * 128 + 128)
                p_ref[head, low : low + 32, cols] = prob.astype(jnp.bfloat16)
            inverse = 1.0 / jnp.sum(total, axis=1, keepdims=True)
            inv_ref[head, low : low + 32, :] = jnp.broadcast_to(inverse, (32, 128))

        return [functools.partial(piece, r) for r in range(0, 2 * BLK, 32)]

    def weave(*lists):
        order = [
            ((n + 0.5) / len(pieces_of), k, piece)
            for k, pieces_of in enumerate(lists)
            for n, piece in enumerate(pieces_of)
        ]
        for _, _, piece in sorted(order, key=lambda entry: entry[:2]):
            piece()

    def scaled_turned(src_ref, dst_ref, b):
        rows = slice(b * BLK, b * BLK + BLK)
        for h in range(2):
            cols = slice(h * HD, h * HD + HD)
            part = src_ref[rows, cols].astype(jnp.float32) * inv_ref[h, rows, :]
            dst_ref[cols, rows] = part.astype(jnp.bfloat16).T

    left = (qt_ref, dot_ref)
    weights = (scale, 1.0)

    def rows_of(kc):
        return range(max(0, kc - blocks), min(blocks - 1, kc) + 1)

    def column_sum(i, kc):
        rows = slice(rows_of(kc)[0] * BLK, rows_of(kc)[-1] * BLK + BLK)
        cols = slice(kc * BLK, (kc + 1) * BLK)
        total = dot(left[i][0:HD, rows], p_ref[0, rows, cols]) + dot(
            left[i][HD : 2 * HD, rows], p_ref[1, rows, cols]
        )
        return total * weights[i] if weights[i] != 1.0 else total

    def back(i, kc):
        cols = pl.ds(kc * BLK, BLK)
        return pltpu.make_async_remote_copy(
            src_ref=ret_send.at[i, :, cols],
            dst_ref=ret_recv.at[i, :, cols],
            send_sem=b_send.at[i, kc],
            recv_sem=b_recv.at[i, kc],
            device_id=(prv, tp),
            device_id_type=MESH,
        )

    pieces = ((1,) * blocks, (blocks // 2,) * 2)

    def straight(i, piece):
        return i == 0 and piece == len(pieces[0]) - 1

    def columns_of(i, piece):
        first = sum(pieces[i][:piece]) * BLK
        return slice(first, first + pieces[i][piece] * BLK)

    def scatter(i, piece, band, target, slot):
        span_of = columns_of(i, piece)
        cols = pl.ds(span_of.start, span_of.stop - span_of.start)
        return pltpu.make_async_remote_copy(
            src_ref=rs_send.at[i, band_of(other(band)), cols],
            dst_ref=rs_recv.at[i, slot, :, cols],
            send_sem=r_send.at[i, piece, slot],
            recv_sem=r_recv.at[i, piece, slot],
            device_id=(ctx, base + other(target)),
            device_id_type=MESH,
        )

    backs = [[back(i, kc) for kc in range(blocks)] for i in range(2)]
    scatters = [
        [[scatter(i, piece, d, d, d - 1) for d in range(1, share)] for piece in range(len(pieces[i]))]
        for i in range(2)
    ]
    relays = [
        [scatter(i, piece, 3, 1, 3) for piece in range(len(pieces[i])) if not straight(i, piece)]
        for i in range(2)
    ]

    def send_piece(i, piece):
        first, second, third = scatters[i][piece]
        if straight(i, piece):
            second.start()
            third.start()
            first.start()
            return

        @pl.when(at_an_end)
        def _():
            relays[i][piece].start()
            second.start()

        pl.when(in_middle)(third.start)
        first.start()

    def add_on_the_way(i, piece):
        cols = columns_of(i, piece)

        @pl.when(in_middle)
        def _():
            relays[i][piece].wait_recv()
            total = total_ref[i, band_of(other(2)), cols]
            total = total + rs_recv[i, 3, :, cols].astype(jnp.float32)
            rs_send[i, band_of(other(2)), cols] = total.astype(jnp.bfloat16)
            scatters[i][piece][1].start()

    def column_back(i, kc):
        ret_send[i, :, kc * BLK : (kc + 1) * BLK] = column_sum(i, kc).astype(jnp.bfloat16)

    def add_returned(i, kc, mine):
        cols = slice(kc * BLK, (kc + 1) * BLK)
        backs[i][kc].wait_recv()
        total = mine + ret_recv[i, :, cols].astype(jnp.float32)
        total_ref[i, :, cols] = total
        rs_send[i, :, cols] = total.astype(jnp.bfloat16)

    def finish(i):
        for piece in range(len(pieces[i])):
            cols = columns_of(i, piece)

            def add_third(piece=piece, cols=cols):
                scatters[i][piece][2].wait_recv()
                total_ref[i, band_of(place), cols] += rs_recv[i, 2, :, cols].astype(jnp.float32)

            if straight(i, piece):
                add_third()
            else:
                pl.when(in_middle)(add_third)
            scatters[i][piece][0].wait_recv()
            scatters[i][piece][1].wait_recv()
        result = total_ref[i, band_of(place), :]
        for d in range(1, share - 1):
            result = result + rs_recv[i, d - 1].astype(jnp.float32)
        (dkt_ref, dvt_ref)[i][...] = result.astype(jnp.bfloat16)

    weave(scores(0, middle(0), span))
    for b in range(blocks):
        ahead = scores(b + 1, middle(b + 1), span) if b + 1 < blocks else []
        weave(ahead, own_max(b))
    for d in range(share):
        forwards[0][d].wait_recv()

    weave(scores(0, 0, middle(0)))
    weave(scores(1, 0, middle(1)), row_max(0))
    for b in range(blocks):
        matrix, vector = [], []
        if b:
            matrix.append(functools.partial(column_back, 1, b - 1))
        if b + 2 < blocks:
            matrix += scores(b + 2, 0, middle(b + 2))
        if b + 1 < blocks:
            vector = row_max(b + 1)
        weave(matrix, vector, probabilities(b))
        scaled_turned(do_ref, dot_ref, b)
        if b:
            backs[1][b - 1].start()
        if b == 2:
            for d in range(1, share):
                gathers[1][d - 1].wait_recv()
                forwards[1][d].start()
            load_kv[1].wait()

    column_back(1, blocks - 1)
    backs[1][blocks - 1].start()
    for kc in range(blocks):
        total_ref[1, :, kc * BLK : (kc + 1) * BLK] = column_sum(1, kc + blocks)
    for b in range(blocks):
        scaled_turned(q_ref, qt_ref, b)
    v_ref[own, :] = kv_ref[1, :, own].T
    for kc in range(blocks):
        add_returned(1, kc, total_ref[1, :, kc * BLK : (kc + 1) * BLK])
        if kc % 2:
            send_piece(1, kc // 2)
    for d in range(share):
        forwards[1][d].wait_recv()
    v_ref[before, :] = kv_ref[1, :, before].T

    def outputs(b):
        rows, window = slice(b * BLK, b * BLK + BLK), slice(b * BLK, b * BLK + span)
        prob = jnp.concatenate([p_ref[0, rows, window], p_ref[1, rows, window]], axis=0)
        sums = dot(prob, v_ref[window, :])
        for h in range(2):
            part = (sums[h * BLK : h * BLK + BLK] * inv_ref[h, rows, :]).astype(jnp.bfloat16)
            out_ref[rows, h * HD : h * HD + HD] = part
            grads = do_ref[rows, h * HD : h * HD + HD].astype(jnp.float32)
            delta = jnp.sum(grads * part.astype(jnp.float32), axis=1, keepdims=True)
            delta_ref[h, rows, :] = jnp.broadcast_to(delta, (BLK, 128))

    def tile_change(b, kc):
        rows, cols = slice(b * BLK, b * BLK + BLK), slice(kc * BLK, kc * BLK + BLK)
        return dot(heads_of(do_ref, rows), kv_ref[1, :, cols])

    def tile_scores(b, kc, change):
        def piece(r):
            cols = slice(kc * BLK, kc * BLK + BLK)
            head, low = r // BLK, r % BLK
            these = slice(b * BLK + low, b * BLK + low + 64)
            delta = delta_ref[head, these, :]
            delta = jnp.concatenate([delta] * (BLK // 128), axis=1)
            held = p_ref[head, these, cols].astype(jnp.float32)
            p_ref[head, these, cols] = (held * (change[r : r + 64] - delta)).astype(jnp.bfloat16)

        return [functools.partial(piece, r) for r in range(0, 2 * BLK, 64)]

    def query_grads(b):
        rows, window = slice(b * BLK, b * BLK + BLK), slice(b * BLK, b * BLK + span)
        dscore = jnp.concatenate([p_ref[0, rows, window], p_ref[1, rows, window]], axis=0)
        sums = dot(dscore, k_ref[window, :])
        for h in range(2):
            part = sums[h * BLK : h * BLK + BLK] * (inv_ref[h, rows, :] * scale)
            dq_ref[rows, h * HD : h * HD + HD] = part.astype(jnp.bfloat16)

    outputs(0)

    tiles = [(b, kc) for kc in range(2 * blocks) for b in rows_of(kc)]
    change = tile_change(*tiles[0])
    column = [None]
    ready = []
    for number, (b, kc) in enumerate(tiles):
        following = [None]
        matrix = []
        if number + 1 < len(tiles):

            def ahead(number=number, following=following):
                following[0] = tile_change(*tiles[number + 1])

            matrix.append(ahead)
        if ready:
            which = ready[0]

            def total(which=which):
                if which < blocks:
                    column_back(0, which)
                else:
                    column[0] = column_sum(0, which)

            matrix.append(total)
            if which < blocks - 1:
                matrix.append(functools.partial(outputs, which + 2)) if which + 2 < blocks else None
        if number == 0:
            matrix.append(functools.partial(outputs, 1))
        weave(matrix, tile_scores(b, kc, change))
        change = following[0]
        if ready:
            which = ready.pop()
            if which < blocks:
                backs[0][which].start()
            else:
                add_returned(0, which - blocks, column[0])
                send_piece(0, which - blocks)
            if which == blocks - 1:
                k_ref[...] = kv_ref[0].T
                for piece in range(len(pieces[1])):
                    add_on_the_way(1, piece)
            if which in (blocks, blocks + 1):
                query_grads(which - blocks)
        if b == rows_of(kc)[-1]:
            ready.append(kc)
    add_returned(0, blocks - 1, column_sum(0, 2 * blocks - 1))
    send_piece(0, blocks - 1)
    for piece in range(blocks - 2):
        add_on_the_way(0, piece)
    query_grads(2)
    add_on_the_way(0, blocks - 2)
    query_grads(3)

    finish(1)
    finish(0)

    always = gathers[1] + forwards[0] + forwards[1] + backs[0] + backs[1]
    middle_only, end_only = [], relays[0] + relays[1]
    for i in range(2):
        for piece, (first, second, third) in enumerate(scatters[i]):
            always += [first, second]
            (always if straight(i, piece) else middle_only).append(third)
    for c in always:
        c.wait_send()

    @pl.when(in_middle)
    def _():
        for c in middle_only:
            c.wait_send()

    @pl.when(at_an_end)
    def _():
        for c in end_only:
            c.wait_send()


def hand_over(*refs):
    count = len(refs) // 2
    sems = refs[-1]
    copies = [
        pltpu.make_async_copy(refs[i], refs[count + i], sems.at[i]) for i in range(count)
    ]
    for c in copies:
        c.start()
    for c in copies:
        c.wait()


def on_device(queries, keys, values, grad_out, doc_lengths, *, n_ctx):
    tokens, width = queries.shape
    columns = keys.shape[1]
    share = HD // columns
    blocks = tokens // BLK
    bf16, f32 = jnp.bfloat16, jnp.float32
    anywhere = pl.BlockSpec(memory_space=pltpu.HBM)
    dma = pltpu.SemaphoreType.DMA
    shapes = [(tokens, width), (tokens, width), (columns, tokens), (columns, tokens)]
    results = pl.pallas_call(
        functools.partial(kernel, n_ctx, tokens, share),
        out_shape=[pltpu.VMEM(shape, bf16) for shape in shapes],
        in_specs=[pl.BlockSpec(memory_space=pltpu.SMEM)] + [anywhere] * 4,
        out_specs=[pl.BlockSpec(memory_space=pltpu.VMEM)] * 4,
        scratch_shapes=[
            pltpu.VMEM((tokens, width), bf16),
            pltpu.VMEM((tokens, width), bf16),
            pltpu.VMEM((width, tokens), bf16),
            pltpu.VMEM((width, tokens), bf16),
            pltpu.VMEM((2, HD, 2 * tokens), bf16),
            pltpu.VMEM((2 * tokens, HD), bf16),
            pltpu.VMEM((2 * tokens, HD), bf16),
            pltpu.VMEM((tokens, tokens + BLK), f32),
            pltpu.VMEM((blocks, 2 * BLK, tokens + BLK), f32),
            pltpu.VMEM((2, tokens, 2 * tokens), bf16),
            pltpu.VMEM((2, tokens, 128), f32),
            pltpu.VMEM((2, tokens, 128), f32),
            pltpu.VMEM((2, tokens, 128), f32),
            pltpu.VMEM((2, HD, tokens), bf16),
            pltpu.VMEM((2, HD, tokens), bf16),
            pltpu.VMEM((2, HD, tokens), f32),
            pltpu.VMEM((2, HD, tokens), bf16),
            pltpu.VMEM((2, share, columns, tokens), bf16),
            dma((4,)),
            dma((2, share - 1)),
            dma((2, share - 1)),
            dma((2, share)),
            dma((2, share)),
            dma((2, blocks)),
            dma((2, blocks)),
            dma((2, blocks, share)),
            dma((2, blocks, share)),
        ],
        compiler_params=pltpu.CompilerParams(
            collective_id=0, has_side_effects=True, vmem_limit_bytes=60 * 1024 * 1024
        ),
        cost_estimate=pl.CostEstimate(
            flops=6 * 2 * 2 * tokens * (tokens + BLK) * HD,
            bytes_accessed=4 * tokens * width * 2,
            transcendentals=2 * tokens * (tokens + BLK),
        ),
    )(doc_lengths, queries, keys.T, values.T, grad_out)
    out, dq, dkt, dvt = pl.pallas_call(
        hand_over,
        out_shape=[jax.ShapeDtypeStruct(shape, bf16) for shape in shapes],
        in_specs=[pl.BlockSpec(memory_space=pltpu.VMEM)] * 4,
        out_specs=[anywhere] * 4,
        scratch_shapes=[dma((4,))],
        compiler_params=pltpu.CompilerParams(vmem_limit_bytes=4 * 1024 * 1024),
        cost_estimate=pl.CostEstimate(
            flops=0, bytes_accessed=2 * tokens * width * 2, transcendentals=0
        ),
    )(*results)
    return out, dq, dkt.T, dvt.T


def solution(mesh):
    in_specs = (P("ctx", "tp"), P("ctx", "tp"), P("ctx", "tp"), P("ctx", "tp"), P())
    out_specs = (P("ctx", "tp"), P("ctx", "tp"), P("ctx", "tp"), P("ctx", "tp"))
    return jax.shard_map(
        functools.partial(on_device, n_ctx=mesh.shape["ctx"]),
        mesh=mesh,
        in_specs=in_specs,
        out_specs=out_specs,
        check_vma=False,
    )
```

```python
import functools
import math

import jax
import jax.numpy as jnp
from jax import lax
from jax.experimental import pallas as pl
from jax.experimental.pallas import tpu as pltpu
from jax.sharding import PartitionSpec as P

HD = 128
BLK = 256
NEG_FILL = -1e30
MESH = pl.DeviceIdType.MESH


def dot(a, b):
    return jnp.dot(a, b, preferred_element_type=jnp.float32)


def dot_rows(a, b):
    return lax.dot_general(a, b, (((1,), (1,)), ((), ())), preferred_element_type=jnp.float32)


def kernel(
    n_ctx,
    tokens,
    share,
    doc_ref,
    q_hbm,
    kt_hbm,
    vt_hbm,
    do_hbm,
    out_ref,
    dq_ref,
    dkt_ref,
    dvt_ref,
    q_ref,
    do_ref,
    qt_ref,
    dot_ref,
    kv_ref,
    bias_ref,
    s_ref,
    p_ref,
    delta_ref,
    max_ref,
    ret_send,
    ret_recv,
    total_ref,
    rs_send,
    rs_recv,
    load_sem,
    g_send,
    g_recv,
    f_send,
    f_recv,
    b_send,
    b_recv,
    r_send,
    r_recv,
):
    scale = 1.0 / math.sqrt(HD)
    factor = scale * math.log2(math.e)
    ctx = lax.axis_index("ctx")
    tp = lax.axis_index("tp")
    place = lax.rem(tp, share)
    base = tp - place
    band = HD // share
    nxt = lax.rem(ctx + 1, n_ctx)
    prv = lax.rem(ctx + n_ctx - 1, n_ctx)
    span = tokens + BLK
    blocks = tokens // BLK
    own = pl.ds(tokens, tokens)
    before = pl.ds(0, tokens)
    kv_hbm = (kt_hbm, vt_hbm)

    def other(d):
        return lax.rem(place + d, share)

    def band_of(index):
        return pl.ds(pl.multiple_of(index * band, band), band)

    load_q = pltpu.make_async_copy(q_hbm, q_ref, load_sem.at[0])
    load_do = pltpu.make_async_copy(do_hbm, do_ref, load_sem.at[1])
    load_kv = [
        pltpu.make_async_copy(
            kv_hbm[i], kv_ref.at[i, band_of(place), own], load_sem.at[2 + i]
        )
        for i in range(2)
    ]
    for c in [load_q, load_do] + load_kv:
        c.start()

    barrier = pltpu.get_barrier_semaphore()
    for d in range(1, share):
        pl.semaphore_signal(
            barrier, inc=1, device_id=(ctx, base + other(d)), device_id_type=MESH
        )
    for c in (nxt, prv):
        pl.semaphore_signal(barrier, inc=1, device_id=(c, tp), device_id_type=MESH)
    pl.semaphore_wait(barrier, share + 1)

    def gather(i):
        copies = [
            pltpu.make_async_remote_copy(
                src_ref=kv_hbm[i],
                dst_ref=kv_ref.at[i, band_of(place), own],
                send_sem=g_send.at[i, d - 1],
                recv_sem=g_recv.at[i, d - 1],
                device_id=(ctx, base + other(d)),
                device_id_type=MESH,
            )
            for d in range(1, share)
        ]
        return copies

    def forward(i, d):
        which = lax.rem(place - d + share, share)
        src = kv_hbm[i] if d == 0 else kv_ref.at[i, band_of(which), own]
        return pltpu.make_async_remote_copy(
            src_ref=src,
            dst_ref=kv_ref.at[i, band_of(which), before],
            send_sem=f_send.at[i, d],
            recv_sem=f_recv.at[i, d],
            device_id=(nxt, tp),
            device_id_type=MESH,
        )

    gathers = [gather(i) for i in range(2)]
    forwards = [[forward(i, d) for d in range(share)] for i in range(2)]

    for c in gathers[0]:
        c.start()
    forwards[0][0].start()

    row_base = ctx * tokens
    window_base = row_base - tokens

    ends = []
    running = doc_ref[0]
    for k in range(1, doc_ref.shape[0]):
        ends.append(running)
        running = running + doc_ref[k]
    lane = lax.broadcasted_iota(jnp.int32, (128, 128), 1)
    sub = lax.broadcasted_iota(jnp.int32, (128, 128), 0)

    def find_start(chunk, carry):
        pos = sub + (row_base + chunk * 128)
        first = jnp.zeros((128, 128), jnp.int32)
        for e in ends:
            first = jnp.where(pos >= e, e, first)
        rows = pl.ds(pl.multiple_of(chunk * 128, 128), 128)
        turn = lax.rem(chunk, BLK // 128) * 128
        begin = first - window_base - lane - (chunk * 128 - turn)
        for j in range(span // 128):
            ok = begin <= j * 128
            if j * 128 >= tokens:
                ok = ok & (lane + (j * 128 - tokens) <= sub + turn)
            bias_ref[rows, j * 128 : j * 128 + 128] = jnp.where(ok, 0.0, NEG_FILL)
        return carry

    lax.fori_loop(0, tokens // 128, find_start, 0)
    load_q.wait()
    qt_ref[...] = q_ref[...].T
    load_do.wait()
    dot_ref[...] = do_ref[...].T

    for c in gathers[0]:
        c.wait_send()
    for c in gathers[1]:
        c.start()
    forwards[1][0].start()
    load_kv[0].wait()
    for d in range(1, share):
        gathers[0][d - 1].wait_recv()
        forwards[0][d].start()

    def heads_of(ref, rows):
        return jnp.concatenate([ref[rows, 0:HD], ref[rows, HD : 2 * HD]], axis=0)

    def middle(b):
        return tokens - b * BLK

    def scores(b, first, last):
        def piece(col):
            rows = slice(b * BLK, b * BLK + BLK)
            cols = slice(b * BLK + col, b * BLK + col + BLK)
            bias = bias_ref[rows, col : col + BLK]
            part = dot(heads_of(q_ref, rows), kv_ref[0, :, cols])
            s_ref[b, 0:BLK, col : col + BLK] = part[0:BLK] + bias
            s_ref[b, BLK : 2 * BLK, col : col + BLK] = part[BLK : 2 * BLK] + bias

        return [functools.partial(piece, col) for col in range(first, last, BLK)]

    def own_max(b):
        def piece(r):
            head, low = r // BLK, b * BLK + r % BLK
            first = middle(b) // 128
            top = s_ref[b, r : r + 32, first * 128 : first * 128 + 128]
            for j in range(first + 1, span // 128):
                top = jnp.maximum(top, s_ref[b, r : r + 32, j * 128 : j * 128 + 128])
            max_ref[head, low : low + 32, :] = top

        return [functools.partial(piece, r) for r in range(0, 2 * BLK, 32)]

    def row_max(b):
        def piece(r):
            head, low = r // BLK, b * BLK + r % BLK
            top = max_ref[head, low : low + 32, :]
            for j in range(middle(b) // 128):
                top = jnp.maximum(top, s_ref[b, r : r + 32, j * 128 : j * 128 + 128])
            top = jnp.max(top, axis=1, keepdims=True)
            max_ref[head, low : low + 32, :] = jnp.broadcast_to(top, (32, 128))

        return [functools.partial(piece, r) for r in range(0, 2 * BLK, 32)]

    def probabilities(b):
        def piece(r):
            head, low = r // BLK, b * BLK + r % BLK
            top = max_ref[head, low : low + 16, :]
            total = jnp.zeros((16, 128), jnp.float32)
            probs = []
            for j in range(span // 128):
                part = s_ref[b, r : r + 16, j * 128 : j * 128 + 128]
                probs.append(jnp.exp2((part - top) * factor))
                total = total + probs[-1]
            inverse = 1.0 / jnp.sum(total, axis=1, keepdims=True)
            for j, prob in enumerate(probs):
                cols = slice(b * BLK + j * 128, b * BLK + j * 128 + 128)
                p_ref[head, low : low + 16, cols] = (prob * inverse).astype(jnp.bfloat16)

        return [functools.partial(piece, r) for r in range(0, 2 * BLK, 16)]

    def weave(*lists):
        order = [
            ((n + 0.5) / len(pieces_of), k, piece)
            for k, pieces_of in enumerate(lists)
            for n, piece in enumerate(pieces_of)
        ]
        for _, _, piece in sorted(order, key=lambda entry: entry[:2]):
            piece()

    left = (qt_ref, dot_ref)
    weights = (scale, 1.0)

    def rows_of(kc):
        return range(max(0, kc - blocks), min(blocks - 1, kc) + 1)

    def column_sum(i, kc):
        rows = slice(rows_of(kc)[0] * BLK, rows_of(kc)[-1] * BLK + BLK)
        cols = slice(kc * BLK, (kc + 1) * BLK)
        total = dot(left[i][0:HD, rows], p_ref[0, rows, cols]) + dot(
            left[i][HD : 2 * HD, rows], p_ref[1, rows, cols]
        )
        return total * weights[i] if weights[i] != 1.0 else total

    def back(i, kc):
        cols = pl.ds(kc * BLK, BLK)
        return pltpu.make_async_remote_copy(
            src_ref=ret_send.at[i, :, cols],
            dst_ref=ret_recv.at[i, :, cols],
            send_sem=b_send.at[i, kc],
            recv_sem=b_recv.at[i, kc],
            device_id=(prv, tp),
            device_id_type=MESH,
        )

    pieces = ((1,) * blocks, (blocks // 2,) * 2)

    def scatter(i, piece, d):
        size = pieces[i][piece] * BLK
        cols = pl.ds(sum(pieces[i][:piece]) * BLK, size)
        return pltpu.make_async_remote_copy(
            src_ref=rs_send.at[i, band_of(other(d)), cols],
            dst_ref=rs_recv.at[i, d - 1, :, cols],
            send_sem=r_send.at[i, piece, d - 1],
            recv_sem=r_recv.at[i, piece, d - 1],
            device_id=(ctx, base + other(d)),
            device_id_type=MESH,
        )

    backs = [[back(i, kc) for kc in range(blocks)] for i in range(2)]
    scatters = [
        [[scatter(i, piece, d) for d in range(1, share)] for piece in range(len(pieces[i]))]
        for i in range(2)
    ]

    def column_back(i, kc):
        ret_send[i, :, kc * BLK : (kc + 1) * BLK] = column_sum(i, kc).astype(jnp.bfloat16)

    def add_returned(i, kc, mine):
        cols = slice(kc * BLK, (kc + 1) * BLK)
        backs[i][kc].wait_recv()
        total = mine + ret_recv[i, :, cols].astype(jnp.float32)
        total_ref[i, :, cols] = total
        rs_send[i, :, cols] = total.astype(jnp.bfloat16)

    def finish(i):
        for piece in scatters[i]:
            for c in piece:
                c.wait_recv()
        result = total_ref[i, band_of(place), :]
        for d in range(1, share):
            result = result + rs_recv[i, d - 1].astype(jnp.float32)
        (dkt_ref, dvt_ref)[i][...] = result.astype(jnp.bfloat16)

    weave(scores(0, middle(0), span))
    for b in range(blocks):
        ahead = scores(b + 1, middle(b + 1), span) if b + 1 < blocks else []
        weave(ahead, own_max(b))
    for d in range(share):
        forwards[0][d].wait_recv()

    weave(scores(0, 0, middle(0)))
    weave(scores(1, 0, middle(1)), row_max(0))
    for b in range(blocks):
        matrix, vector = [], []
        if b:
            matrix.append(functools.partial(column_back, 1, b - 1))
        if b + 2 < blocks:
            matrix += scores(b + 2, 0, middle(b + 2))
        if b + 1 < blocks:
            vector = row_max(b + 1)
        weave(matrix, vector, probabilities(b))
        if b:
            backs[1][b - 1].start()
        if b == 2:
            for d in range(1, share):
                gathers[1][d - 1].wait_recv()
                forwards[1][d].start()
            load_kv[1].wait()

    column_back(1, blocks - 1)
    backs[1][blocks - 1].start()
    for kc in range(blocks):
        total_ref[1, :, kc * BLK : (kc + 1) * BLK] = column_sum(1, kc + blocks)
    for kc in range(blocks):
        add_returned(1, kc, total_ref[1, :, kc * BLK : (kc + 1) * BLK])
        if kc % 2:
            for c in scatters[1][kc // 2]:
                c.start()
    for d in range(share):
        forwards[1][d].wait_recv()

    def outputs(b):
        rows, window = slice(b * BLK, b * BLK + BLK), slice(b * BLK, b * BLK + span)
        prob = jnp.concatenate([p_ref[0, rows, window], p_ref[1, rows, window]], axis=0)
        sums = dot_rows(prob, kv_ref[1, :, window])
        for h in range(2):
            part = sums[h * BLK : h * BLK + BLK].astype(jnp.bfloat16)
            out_ref[rows, h * HD : h * HD + HD] = part
            grads = do_ref[rows, h * HD : h * HD + HD].astype(jnp.float32)
            delta = jnp.sum(grads * part.astype(jnp.float32), axis=1, keepdims=True)
            delta_ref[h, rows, :] = jnp.broadcast_to(delta, (BLK, 128))

    def tile_change(b, kc):
        rows, cols = slice(b * BLK, b * BLK + BLK), slice(kc * BLK, kc * BLK + BLK)
        return dot(heads_of(do_ref, rows), kv_ref[1, :, cols])

    def tile_scores(b, kc, change):
        def piece(r):
            cols = slice(kc * BLK, kc * BLK + BLK)
            head, low = r // BLK, r % BLK
            these = slice(b * BLK + low, b * BLK + low + 64)
            delta = delta_ref[head, these, :]
            delta = jnp.concatenate([delta] * (BLK // 128), axis=1)
            held = p_ref[head, these, cols].astype(jnp.float32)
            p_ref[head, these, cols] = (held * (change[r : r + 64] - delta)).astype(jnp.bfloat16)

        return [functools.partial(piece, r) for r in range(0, 2 * BLK, 64)]

    def query_grads(b):
        rows, window = slice(b * BLK, b * BLK + BLK), slice(b * BLK, b * BLK + span)
        dscore = jnp.concatenate([p_ref[0, rows, window], p_ref[1, rows, window]], axis=0)
        sums = dot_rows(dscore, kv_ref[0, :, window])
        for h in range(2):
            part = sums[h * BLK : h * BLK + BLK] * scale
            dq_ref[rows, h * HD : h * HD + HD] = part.astype(jnp.bfloat16)

    outputs(0)

    tiles = [(b, kc) for kc in range(2 * blocks) for b in rows_of(kc)]
    change = tile_change(*tiles[0])
    column = [None]
    ready = []
    for number, (b, kc) in enumerate(tiles):
        following = [None]
        matrix = []
        if number + 1 < len(tiles):

            def ahead(number=number, following=following):
                following[0] = tile_change(*tiles[number + 1])

            matrix.append(ahead)
        if ready:
            which = ready[0]

            def total(which=which):
                if which < blocks:
                    column_back(0, which)
                else:
                    column[0] = column_sum(0, which)

            matrix.append(total)
            if which < blocks - 1:
                matrix.append(functools.partial(outputs, which + 2)) if which + 2 < blocks else None
        if number == 0:
            matrix.append(functools.partial(outputs, 1))
        weave(matrix, tile_scores(b, kc, change))
        change = following[0]
        if ready:
            which = ready.pop()
            if which < blocks:
                backs[0][which].start()
            else:
                add_returned(0, which - blocks, column[0])
                for c in scatters[0][which - blocks]:
                    c.start()
            if which in (blocks, blocks + 1):
                query_grads(which - blocks)
        if b == rows_of(kc)[-1]:
            ready.append(kc)
    add_returned(0, blocks - 1, column_sum(0, 2 * blocks - 1))
    for c in scatters[0][blocks - 1]:
        c.start()

    finish(1)

    for b in range(2, blocks):
        query_grads(b)

    finish(0)

    for i in range(2):
        for c in (gathers[i] if i else []) + forwards[i] + backs[i] + sum(scatters[i], []):
            c.wait_send()


def hand_over(*refs):
    count = len(refs) // 2
    sems = refs[-1]
    copies = [
        pltpu.make_async_copy(refs[i], refs[count + i], sems.at[i]) for i in range(count)
    ]
    for c in copies:
        c.start()
    for c in copies:
        c.wait()


def on_device(queries, keys, values, grad_out, doc_lengths, *, n_ctx):
    tokens, width = queries.shape
    columns = keys.shape[1]
    share = HD // columns
    blocks = tokens // BLK
    bf16, f32 = jnp.bfloat16, jnp.float32
    anywhere = pl.BlockSpec(memory_space=pltpu.HBM)
    dma = pltpu.SemaphoreType.DMA
    shapes = [(tokens, width), (tokens, width), (columns, tokens), (columns, tokens)]
    results = pl.pallas_call(
        functools.partial(kernel, n_ctx, tokens, share),
        out_shape=[pltpu.VMEM(shape, bf16) for shape in shapes],
        in_specs=[pl.BlockSpec(memory_space=pltpu.SMEM)] + [anywhere] * 4,
        out_specs=[pl.BlockSpec(memory_space=pltpu.VMEM)] * 4,
        scratch_shapes=[
            pltpu.VMEM((tokens, width), bf16),
            pltpu.VMEM((tokens, width), bf16),
            pltpu.VMEM((width, tokens), bf16),
            pltpu.VMEM((width, tokens), bf16),
            pltpu.VMEM((2, HD, 2 * tokens), bf16),
            pltpu.VMEM((tokens, tokens + BLK), f32),
            pltpu.VMEM((blocks, 2 * BLK, tokens + BLK), f32),
            pltpu.VMEM((2, tokens, 2 * tokens), bf16),
            pltpu.VMEM((2, tokens, 128), f32),
            pltpu.VMEM((2, tokens, 128), f32),
            pltpu.VMEM((2, HD, tokens), bf16),
            pltpu.VMEM((2, HD, tokens), bf16),
            pltpu.VMEM((2, HD, tokens), f32),
            pltpu.VMEM((2, HD, tokens), bf16),
            pltpu.VMEM((2, share - 1, columns, tokens), bf16),
            dma((4,)),
            dma((2, share - 1)),
            dma((2, share - 1)),
            dma((2, share)),
            dma((2, share)),
            dma((2, blocks)),
            dma((2, blocks)),
            dma((2, blocks, share - 1)),
            dma((2, blocks, share - 1)),
        ],
        compiler_params=pltpu.CompilerParams(
            collective_id=0, has_side_effects=True, vmem_limit_bytes=60 * 1024 * 1024
        ),
        cost_estimate=pl.CostEstimate(
            flops=6 * 2 * 2 * tokens * (tokens + BLK) * HD,
            bytes_accessed=4 * tokens * width * 2,
            transcendentals=2 * tokens * (tokens + BLK),
        ),
    )(doc_lengths, queries, keys.T, values.T, grad_out)
    out, dq, dkt, dvt = pl.pallas_call(
        hand_over,
        out_shape=[jax.ShapeDtypeStruct(shape, bf16) for shape in shapes],
        in_specs=[pl.BlockSpec(memory_space=pltpu.VMEM)] * 4,
        out_specs=[anywhere] * 4,
        scratch_shapes=[dma((4,))],
        compiler_params=pltpu.CompilerParams(vmem_limit_bytes=4 * 1024 * 1024),
        cost_estimate=pl.CostEstimate(
            flops=0, bytes_accessed=2 * tokens * width * 2, transcendentals=0
        ),
    )(*results)
    return out, dq, dkt.T, dvt.T


def solution(mesh):
    in_specs = (P("ctx", "tp"), P("ctx", "tp"), P("ctx", "tp"), P("ctx", "tp"), P())
    out_specs = (P("ctx", "tp"), P("ctx", "tp"), P("ctx", "tp"), P("ctx", "tp"))
    return jax.shard_map(
        functools.partial(on_device, n_ctx=mesh.shape["ctx"]),
        mesh=mesh,
        in_specs=in_specs,
        out_specs=out_specs,
        check_vma=False,
    )
```
